256 devices in a mesh: modes: 8 (over y, core), elems: 32 (over z, x).
Axes of the slice: x: 4, y: 4, z: 8, core: 2. Of those that a mesh axis runs over, the one named last changes fastest.
Arguments:
- adjoint_modes: float32 [3, 512, 41472], P(None, 'modes', 'elems'), may hold values from -3 to 3
- base_planes: float32 [3, 8, 5184, 512], P(None, 'modes', 'elems'), may hold values from -8 to 8
- metrics: float32 [4, 512], P(None, 'elems'), may hold values from -0.12 to 0.12
- send_point: int32 [32, 32, 64], P('elems'), may hold values from 0 to 1295
- dest_node: int32 [32, 32, 64], P('elems'), may hold values from 0 to 511
- pair_counts: int32 [32, 32], P('elems'), may hold values from 0 to 64, as said below
Outputs:
- advection: float32 [3, 512, 41472], P(None, 'modes', 'elems')
- shared_totals: float32 [3, 512, 16384], P(None, 'modes', 'elems')
The draws below stay inside these ranges and needn't reach their ends.
Inputs may be any that keep to these rules, and one draw needn't show every extreme that they name: `send_point`: a point of the source partition, numbered within its 16 elements. `pair_counts`: in every draw some owner gets 64 live slots from every source partition.
All inputs are finite; a program needn't handle non-finite values.
Results may differ from the reference program's by a relative error of at most 0.0003.
Values sent between devices are 32-bit elements; how exact they have to be, the bound alone decides.
A program may use at most 128 MiB of HBM per device.

```python
import math
import jax
import jax.numpy as jnp
import numpy as np
from jax import lax

NP = 9
NZ = 512
E_DEV = 16
BLOCK = 64
NODES_OWN = 512
ELEMS = 512
NPTS = 41472
N_MODES = 8
N_ELEMS = 32


def spectrum(power):
    position = jnp.arange(NZ, dtype=jnp.int32)
    wavenumber = jnp.where(position == 1, NZ // 2, position // 2).astype(jnp.float32)
    return 0.3 / (1.0 + wavenumber / 8.0) ** power


def draw_adjoint_modes(key, part):
    key = jax.random.fold_in(key, 11)
    shape_all = (3, NZ, NPTS)
    profile = spectrum(1.5)[None, :, None]
    return jax.random.normal(key, shape_all, jnp.float32) * profile


def wave_sum(key, count, strength, decay, level):
    shape_pts = (3, N_MODES, NPTS // N_MODES, 1)
    offsets = jnp.array([level, 0.0, 0.0], jnp.float32).reshape(3, 1, 1, 1)
    total = offsets + jax.random.uniform(key, shape_pts, jnp.float32, -0.3, 0.3)
    plane_idx = jnp.arange(NZ, dtype=jnp.int32)
    for degree in range(1, count + 1):
        sized = jax.random.normal(jax.random.fold_in(key, degree), shape_pts, jnp.float32) * (strength / degree ** decay)
        shift = jax.random.uniform(jax.random.fold_in(key, 100 + degree), shape_pts, jnp.float32, 0.0, 2.0 * math.pi)
        angles = 2.0 * math.pi / NZ * (degree * plane_idx % NZ).astype(jnp.float32)
        total = total + sized * jnp.cos(angles + shift)
    return total


def draw_base_planes(key, part):
    key = jax.random.fold_in(key, 23)
    shape_full = (3, N_MODES, NPTS // N_MODES, NZ)
    smooth = wave_sum(key, min(6, NZ // 2 - 1), 0.3, 1.0, 0.8)
    rough = jax.random.normal(jax.random.fold_in(key, 500), shape_full, jnp.float32) * 0.03
    return smooth + rough


def draw_pair_counts(key, part):
    key = jax.random.fold_in(key, 37)
    counts = jax.random.randint(key, (N_ELEMS, N_ELEMS), 0, BLOCK + 1)
    full_owner = jax.random.randint(jax.random.fold_in(key, 1), (), 0, N_ELEMS)
    columns = jnp.arange(N_ELEMS, dtype=jnp.int32)[None, :]
    return jnp.where(columns == full_owner, BLOCK, counts).astype(jnp.int32)


def place_ends(drawn, rng, smallest, high):
    spot = [jax.random.randint(jax.random.fold_in(rng, axis), (), 0, length) for axis, length in enumerate(drawn.shape)]
    widest = drawn.shape.index(max(drawn.shape))
    beside = spot[:widest] + [(spot[widest] + 1) % drawn.shape[widest]] + spot[widest + 1:]
    return drawn.at[tuple(spot)].set(smallest).at[tuple(beside)].set(high)


def levels(stream_key, dims, shards, smallest, largest):
    loudness = 1.0
    for dim, shards_of in shards:
        heights = jax.random.uniform(jax.random.fold_in(jax.random.fold_in(stream_key, 6), dim), (shards_of,), jnp.float32, smallest / len(shards), largest / len(shards))
        loudness = loudness * jnp.repeat(jnp.exp(heights), dims[dim] // shards_of).reshape((-1,) + (1,) * (len(dims) - 1 - dim))
    return loudness


def setup_inputs(seed: int = 0) -> dict:
    arg_keys = jax.random.split(jax.random.key(seed), 7)
    return {
        "adjoint_modes": draw_adjoint_modes(jax.random.fold_in(arg_keys[6], 71), 0),
        "base_planes": draw_base_planes(jax.random.fold_in(arg_keys[6], 71), 0),
        "metrics": jnp.clip(jax.random.uniform(arg_keys[2], (4, ELEMS), jnp.float32, -0.12, 0.12) * levels(arg_keys[2], (4, ELEMS), ((1, 32),), -0.4, 0.0), -0.12, 0.12),
        "send_point": place_ends(jax.random.randint(arg_keys[3], (N_ELEMS, N_ELEMS, BLOCK), 0, E_DEV * NP * NP), jax.random.fold_in(arg_keys[3], 1), 0, (E_DEV * NP * NP) - 1).astype(jnp.int32),
        "dest_node": place_ends(jax.random.randint(arg_keys[4], (N_ELEMS, N_ELEMS, BLOCK), 0, NODES_OWN), jax.random.fold_in(arg_keys[4], 1), 0, NODES_OWN - 1).astype(jnp.int32),
        "pair_counts": draw_pair_counts(jax.random.fold_in(arg_keys[6], 71), 0),
    }


span_wavenumber = 0.4


def chebyshev_table(count):
    degree = count - 1
    position = np.arange(count)
    node_x = np.cos(np.pi * position / degree)
    weights = np.where((position == 0) | (position == degree), 2.0, 1.0)
    sign_terms = (-1.0) ** position
    identity = np.eye(count)
    spacing = node_x[:, None] - node_x[None, :] + identity
    matrix = (weights[:, None] * sign_terms[:, None]) / (weights[None, :] * sign_terms[None, :]) / spacing
    matrix = matrix * (1.0 - identity)
    matrix = matrix - identity * matrix.sum(axis=1)[:, None]
    return jnp.asarray(matrix, dtype=jnp.float32)


def spectral_tables(planes):
    position = jnp.arange(planes, dtype=jnp.int32)
    wavenumber = jnp.where(position == 1, planes // 2, position // 2).astype(jnp.int32)
    phase_idx = (position[:, None] * wavenumber[None, :]) % planes
    angles = (2.0 * math.pi / planes) * phase_idx.astype(jnp.float32)
    sine_col = (position % 2 == 1) & (position != 1)
    synth_table = jnp.where(sine_col[None, :], jnp.sin(angles), jnp.cos(angles))
    weighting = jnp.where(position <= 1, 1.0, 2.0).astype(jnp.float32) / planes
    analysis = jnp.transpose(synth_table) * weighting[:, None]
    speeds = span_wavenumber * wavenumber.astype(jnp.float32)
    slope_table = jnp.where(position[None, :] <= 1, 0.0,
                            jnp.where(sine_col[None, :], speeds[None, :] * jnp.cos(angles),
                                      -speeds[None, :] * jnp.sin(angles)))
    return synth_table, analysis, slope_table


def plane_gradient(field_in, metric, diff_table):
    precise = lax.Precision.HIGHEST
    components, points, planes = field_in.shape
    elements = metric.shape[1]
    edge_count = diff_table.shape[0]
    shaped = field_in.reshape(components, elements, edge_count, edge_count, planes)
    along_xi = jnp.einsum("ai,ceijz->ceajz", diff_table, shaped, precision=precise)
    along_eta = jnp.einsum("bj,ceijz->ceibz", diff_table, shaped, precision=precise)

    def combine_rows(row_xi, row_eta):
        mixed = row_xi[None, :, None, None, None] * along_xi + row_eta[None, :, None, None, None] * along_eta
        return mixed.reshape(components, points, planes)

    return combine_rows(metric[0], metric[1]), combine_rows(metric[2], metric[3])


def advect_points(coefficients, base_flow, metric, synth_table, analysis, dz_matrix, slope_table, diff_table):
    precise = lax.Precision.HIGHEST
    velocity = jnp.einsum("ckp,zk->cpz", coefficients, synth_table, precision=precise)
    along_z = jnp.einsum("ckp,zk->cpz", coefficients, slope_table, precision=precise)
    base_z = jnp.einsum("cpw,zw->cpz", base_flow, dz_matrix, precision=precise)
    velocity_x, velocity_y = plane_gradient(velocity, metric, diff_table)
    flow_x, flow_y = plane_gradient(base_flow, metric, diff_table)
    grads_vel = (velocity_x, velocity_y, along_z)
    grads_base = (flow_x, flow_y, base_z)
    outputs = []
    for comp_out in range(3):
        summed = jnp.zeros_like(velocity[0])
        for comp_in in range(3):
            summed = summed - base_flow[comp_in] * grads_vel[comp_in][comp_out] + velocity[comp_in] * grads_base[comp_out][comp_in]
        outputs.append(summed)
    physical = jnp.stack(outputs)
    return jnp.einsum("cpz,kz->ckp", physical, analysis, precision=precise)


def reference(adjoint_modes, base_planes, metrics, send_point, dest_node, pair_counts):
    precise = lax.Precision.HIGHEST
    synth_table, analysis, slope_table = spectral_tables(NZ)
    dz_matrix = jnp.dot(slope_table, analysis, precision=precise)
    diff_table = chebyshev_table(NP)
    sub_elems = E_DEV // N_MODES
    sub_points = sub_elems * NP * NP
    block_count = N_ELEMS * N_MODES

    def one_block(block):
        block = block.astype(jnp.int32)
        owner_part = (block // N_MODES).astype(jnp.int32)
        piece = (block % N_MODES).astype(jnp.int32)
        zero_idx = jnp.zeros((), jnp.int32)
        point_start = (block * sub_points).astype(jnp.int32)
        coefficients = lax.dynamic_slice_in_dim(adjoint_modes, point_start, sub_points, 2)
        base_start = (owner_part * sub_points).astype(jnp.int32)
        base_flow = lax.dynamic_slice(base_planes, (zero_idx, piece, base_start, zero_idx), (3, 1, sub_points, NZ))[:, 0]
        elem_start = (block * sub_elems).astype(jnp.int32)
        metric = lax.dynamic_slice_in_dim(metrics, elem_start, sub_elems, 1)
        return advect_points(coefficients, base_flow, metric, synth_table, analysis, dz_matrix, slope_table, diff_table)

    stacked = lax.map(one_block, jnp.arange(block_count, dtype=jnp.int32))
    advection = jnp.transpose(stacked, (1, 2, 0, 3)).reshape(3, NZ, NPTS)
    rows_all = 3 * NZ
    flat_rows = advection.reshape(rows_all, NPTS)
    part_points = E_DEV * NP * NP
    slots = jnp.arange(BLOCK, dtype=jnp.int32)
    owners = jnp.arange(N_ELEMS, dtype=jnp.int32)

    def add_source(totals, source):
        points = (source * part_points + send_point[source]).astype(jnp.int32)
        live_slots = slots[None, :] < pair_counts[source][:, None]
        picked = flat_rows[:, points.reshape(-1)].reshape(rows_all, N_ELEMS, BLOCK)
        picked = jnp.where(live_slots[None], picked, 0.0)
        target = (owners[:, None] * NODES_OWN + dest_node[source]).astype(jnp.int32)
        totals = totals.at[:, target.reshape(-1)].add(picked.reshape(rows_all, N_ELEMS * BLOCK))
        return totals, None

    initial = jnp.zeros((rows_all, N_ELEMS * NODES_OWN), jnp.float32)
    totals, unused = lax.scan(add_source, initial, jnp.arange(N_ELEMS, dtype=jnp.int32))
    return advection, totals.reshape(3, NZ, N_ELEMS * NODES_OWN)
```

```python
import math

import jax
import jax.numpy as jnp
import numpy as np
from jax import lax
from jax.sharding import PartitionSpec as P

NP = 9
NODES_OWN = 512


span_wavenumber = 0.4


def chebyshev_table(count):
    degree = count - 1
    position = np.arange(count)
    node_x = np.cos(np.pi * position / degree)
    weights = np.where((position == 0) | (position == degree), 2.0, 1.0)
    sign_terms = (-1.0) ** position
    identity = np.eye(count)
    spacing = node_x[:, None] - node_x[None, :] + identity
    matrix = (
        weights[:, None] * sign_terms[:, None] / (weights[None, :] * sign_terms[None, :]) / spacing
    )
    matrix = matrix * (1.0 - identity)
    matrix = matrix - identity * matrix.sum(axis=1)[:, None]
    return jnp.asarray(matrix, dtype=jnp.float32)


def spectral_tables(planes):
    position = np.arange(planes)
    wavenumber = np.where(position == 1, planes // 2, position // 2)
    angles = 2.0 * np.pi / planes * (position[:, None] * wavenumber[None, :] % planes)
    sine_col = (position % 2 == 1) & (position != 1)
    synth_table = np.where(sine_col[None, :], np.sin(angles), np.cos(angles))
    weighting = np.where(position <= 1, 1.0, 2.0) / planes
    analysis = synth_table.T * weighting[:, None]
    speeds = span_wavenumber * wavenumber
    slope_table = np.where(
        position[None, :] <= 1,
        0.0,
        np.where(
            sine_col[None, :], speeds[None, :] * np.cos(angles), -speeds[None, :] * np.sin(angles)
        ),
    )
    dz_matrix = slope_table @ analysis
    return tuple(t.astype(np.float32) for t in (synth_table, analysis, slope_table, dz_matrix))


def plane_gradient(field_in, metric, diff_table):
    precise = lax.Precision.HIGH
    components, points, planes = field_in.shape
    elements = metric.shape[1]
    edge_count = diff_table.shape[0]
    shaped = field_in.reshape(components, elements, edge_count, edge_count, planes)
    along_xi = jnp.einsum("ai,ceijz->ceajz", diff_table, shaped, precision=precise)
    along_eta = jnp.einsum("bj,ceijz->ceibz", diff_table, shaped, precision=precise)

    def combine_rows(row_xi, row_eta):
        mixed = (
            row_xi[None, :, None, None, None] * along_xi
            + row_eta[None, :, None, None, None] * along_eta
        )
        return mixed.reshape(components, points, planes)

    return (combine_rows(metric[0], metric[1]), combine_rows(metric[2], metric[3]))


def advect_points(
    coefficients, base_flow, metric, synth_table, analysis, dz_matrix, slope_table, diff_table
):
    precise = lax.Precision.HIGH
    velocity = jnp.einsum("ckp,zk->cpz", coefficients, synth_table, precision=precise)
    along_z = jnp.einsum("ckp,zk->cpz", coefficients, slope_table, precision=precise)
    base_z = jnp.einsum("cpw,zw->cpz", base_flow, dz_matrix, precision=precise)
    velocity_x, velocity_y = plane_gradient(velocity, metric, diff_table)
    flow_x, flow_y = plane_gradient(base_flow, metric, diff_table)
    grads_vel = (velocity_x, velocity_y, along_z)
    grads_base = (flow_x, flow_y, base_z)
    outputs = []
    for comp_out in range(3):
        summed = jnp.zeros_like(velocity[0])
        for comp_in in range(3):
            summed = (
                summed
                - base_flow[comp_in] * grads_vel[comp_in][comp_out]
                + velocity[comp_in] * grads_base[comp_out][comp_in]
            )
        outputs.append(summed)
    physical = jnp.stack(outputs)
    return jnp.einsum("cpz,kz->ckp", physical, analysis, precision=precise)


def per_device(adjoint_modes, base_planes, metrics, send_point, dest_node, pair_counts):
    precise = lax.Precision.HIGH
    components, local_coefs, local_points = adjoint_modes.shape
    planes = base_planes.shape[3]
    groups = lax.axis_size("modes")
    sub_points = local_points // groups
    sub_elems = sub_points // (NP * NP)
    synth_table, analysis, slope_table, dz_matrix = spectral_tables(planes)
    diff_table = chebyshev_table(NP)
    coefficients = lax.all_to_all(adjoint_modes, "modes", split_axis=2, concat_axis=1, tiled=True)
    first_elem = lax.axis_index("modes") * sub_elems
    metric = lax.dynamic_slice_in_dim(metrics, first_elem, sub_elems, 1)
    result = advect_points(
        coefficients,
        base_planes[:, 0],
        metric,
        synth_table,
        analysis,
        dz_matrix,
        slope_table,
        diff_table,
    )
    advection = lax.all_to_all(result, "modes", split_axis=1, concat_axis=2, tiled=True)
    rows_all = components * local_coefs
    flat_rows = advection.reshape(rows_all, local_points)
    partners = send_point.shape[1]
    slot_count = send_point.shape[2]
    live_slots = jnp.arange(slot_count, dtype=jnp.int32)[None, :] < pair_counts[0][:, None]
    sent_from = jnp.where(live_slots, send_point[0], -1).reshape(-1)
    sent_to = jnp.where(live_slots, dest_node[0], -1)
    pick_table = (
        jnp.arange(local_points, dtype=jnp.int32)[:, None] == sent_from[None, :]
    ).astype(jnp.float32)
    picked = jnp.dot(flat_rows, pick_table, precision=precise)
    picked = picked.reshape(rows_all, partners, slot_count)
    arrived = lax.all_to_all(picked, "elems", split_axis=1, concat_axis=1, tiled=True)
    nodes = lax.all_to_all(sent_to, "elems", split_axis=0, concat_axis=0, tiled=True)
    node_table = (
        nodes.reshape(-1)[:, None] == jnp.arange(NODES_OWN, dtype=jnp.int32)[None, :]
    ).astype(jnp.float32)
    totals = jnp.dot(arrived.reshape(rows_all, -1), node_table, precision=precise)
    return (advection, totals.reshape(components, local_coefs, NODES_OWN))


def solution(mesh):
    return jax.shard_map(
        per_device,
        mesh=mesh,
        in_specs=(
            P(None, "modes", "elems"),
            P(None, "modes", "elems", None),
            P(None, "elems"),
            P("elems", None, None),
            P("elems", None, None),
            P("elems", None),
        ),
        out_specs=(P(None, "modes", "elems"), P(None, "modes", "elems")),
        check_vma=False,
    )
```

```python
import jax
import jax.numpy as jnp
import numpy as np
from jax import lax
from jax.experimental import pallas as pl
from jax.experimental.pallas import tpu as pltpu
from jax.sharding import PartitionSpec as P

NP = 9
NODES_OWN = 512
MESH = pl.DeviceIdType.MESH
F32 = jnp.float32
BF16 = jnp.bfloat16

span_wavenumber = 0.4


def chebyshev_table(count):
    degree = count - 1
    position = np.arange(count)
    node_x = np.cos(np.pi * position / degree)
    weights = np.where((position == 0) | (position == degree), 2.0, 1.0)
    sign_terms = (-1.0) ** position
    identity = np.eye(count)
    spacing = node_x[:, None] - node_x[None, :] + identity
    matrix = (
        weights[:, None] * sign_terms[:, None] / (weights[None, :] * sign_terms[None, :]) / spacing
    )
    matrix = matrix * (1.0 - identity)
    matrix = matrix - identity * matrix.sum(axis=1)[:, None]
    return matrix


def spectral_tables(planes):
    position = np.arange(planes)
    wavenumber = np.where(position == 1, planes // 2, position // 2)
    angles = 2.0 * np.pi / planes * (position[:, None] * wavenumber[None, :] % planes)
    sine_col = (position % 2 == 1) & (position != 1)
    synth_table = np.where(sine_col[None, :], np.sin(angles), np.cos(angles))
    weighting = np.where(position <= 1, 1.0, 2.0) / planes
    analysis = synth_table.T * weighting[:, None]
    speeds = span_wavenumber * wavenumber
    slope_table = np.where(
        position[None, :] <= 1,
        0.0,
        np.where(
            sine_col[None, :], speeds[None, :] * np.cos(angles), -speeds[None, :] * np.sin(angles)
        ),
    )
    return synth_table, analysis, slope_table, slope_table @ analysis


def halves_of(table):
    single = table.astype(np.float32)
    high = single.astype(BF16)
    low = (single - high.astype(np.float32)).astype(BF16)
    return high, low


def gradient_tables(sub_elems, width):
    diff = chebyshev_table(NP)
    points = sub_elems * NP * NP
    tables = np.zeros((2, width, width), np.float32)
    along = (np.kron(diff, np.eye(NP)), np.kron(np.eye(NP), diff))
    for direction in range(2):
        for elem in range(sub_elems):
            rows = slice(elem * NP * NP, (elem + 1) * NP * NP)
            tables[direction, rows, rows] = along[direction].T
    assert points <= width
    return tables


def split(value):
    high = value.astype(BF16)
    return high, (value - high.astype(F32)).astype(BF16)


def dot(left, right):
    return jnp.dot(left, right, preferred_element_type=F32)


def dot3(left_high, left_low, right_high, right_low):
    return dot(left_high, right_high) + (dot(left_high, right_low) + dot(left_low, right_high))


def dot6(left, right):
    return jnp.dot(left, right, precision=lax.Precision.HIGHEST, preferred_element_type=F32)


def body(
    groups,
    partners,
    points,
    x_hbm,
    base_hbm,
    metrics,
    picks,
    nodes,
    synth_high_hbm,
    synth_low_hbm,
    dz_hbm,
    analysis_high_hbm,
    analysis_low_hbm,
    grad_hbm,
    advection_hbm,
    totals_hbm,
    x_v,
    base_v,
    synth_high,
    synth_low,
    dz,
    analysis_high,
    analysis_low,
    grad_tables,
    stage_a,
    stage_b,
    coef_a,
    coef_b,
    padded,
    base_t,
    base_z,
    flow_xy,
    grad_high,
    grad_low,
    pick_table,
    node_rows,
    node_table,
    node_in,
    vel,
    along_z,
    vel_xy,
    phys_high,
    phys_low,
    adv,
    send_adv,
    recv_adv,
    advection,
    adv_parts,
    send_slots,
    recv_slots,
    slot_parts,
    totals,
    load_sem,
    store_sem,
    a_send,
    a_recv,
    b_send,
    b_recv,
    adv_send,
    adv_recv,
    node_send,
    node_recv,
    slot_send,
    slot_recv,
):
    me = lax.axis_index("modes")
    part = lax.axis_index("elems")
    planes = dz.shape[0]
    coefs = planes // groups
    extra = points - 128
    pairs = partners // 2
    full = groups * points

    loads = [
        pltpu.make_async_copy(source, target, load_sem.at[i])
        for i, (source, target) in enumerate(
            (
                (x_hbm, x_v),
                (base_hbm, base_v),
                (grad_hbm, grad_tables),
                (dz_hbm, dz),
                (synth_high_hbm, synth_high),
                (synth_low_hbm, synth_low),
                (analysis_high_hbm, analysis_high),
                (analysis_low_hbm, analysis_low),
            )
        )
    ]
    for load in loads:
        load.start()

    barrier = pltpu.get_barrier_semaphore()

    def group_peer(d):
        return lax.rem(me + d, groups)

    def part_peer(d):
        return lax.rem(part + d, partners)

    def greet_group(d, carry):
        pl.semaphore_signal(barrier, inc=1, device_id=(group_peer(d), part), device_id_type=MESH)
        return carry

    def greet_part(d, carry):
        pl.semaphore_signal(barrier, inc=1, device_id=(me, part_peer(d)), device_id_type=MESH)
        return carry

    lax.fori_loop(1, groups, greet_group, 0)
    lax.fori_loop(1, partners, greet_part, 0)

    loads[0].wait()
    for g in range(groups):
        first = g * points
        stage_a[g, :, 0:128] = x_v[0, :, first : first + 128]
        stage_a[g, :, 128:256] = x_v[1, :, first : first + 128]
        stage_b[g, :, 0:128] = x_v[2, :, first : first + 128]
        rest = [x_v[c, :, first + 128 : first + points] for c in range(3)]
        rest.append(jnp.zeros((coefs, 128 - 3 * extra), F32))
        stage_b[g, :, 128:256] = jnp.concatenate(rest, axis=1)

    pl.semaphore_wait(barrier, groups - 1 + partners - 1)

    def group_copy(source, target, send, recv, to, slot):
        return pltpu.make_async_remote_copy(
            src_ref=source,
            dst_ref=target,
            send_sem=send.at[slot],
            recv_sem=recv.at[me],
            device_id=(to, part),
            device_id_type=MESH,
        )

    def group_arrival(target, send, recv, origin):
        return pltpu.make_async_remote_copy(
            src_ref=target,
            dst_ref=target,
            send_sem=send.at[origin],
            recv_sem=recv.at[origin],
            device_id=(origin, part),
            device_id_type=MESH,
        )

    def send_a(d, carry):
        to = group_peer(d)
        group_copy(stage_a.at[to], coef_a.at[me], a_send, a_recv, to, to).start()
        return carry

    def send_b(d, carry):
        to = group_peer(d)
        group_copy(stage_b.at[to], coef_b.at[me], b_send, b_recv, to, to).start()
        return carry

    lax.fori_loop(1, groups, send_a, 0)
    lax.fori_loop(1, groups, send_b, 0)
    coef_a[me] = stage_a[me]
    coef_b[me] = stage_b[me]

    def part_copy(source, target, send, recv, to):
        return pltpu.make_async_remote_copy(
            src_ref=source,
            dst_ref=target,
            send_sem=send.at[to],
            recv_sem=recv.at[part],
            device_id=(me, to),
            device_id_type=MESH,
        )

    def part_arrival(target, send, recv, origin):
        return pltpu.make_async_remote_copy(
            src_ref=target,
            dst_ref=target,
            send_sem=send.at[origin],
            recv_sem=recv.at[origin],
            device_id=(me, origin),
            device_id_type=MESH,
        )

    def send_nodes(d, carry):
        to = part_peer(d)
        part_copy(nodes.at[to], node_in.at[part], node_send, node_recv, to).start()
        return carry

    lax.fori_loop(1, partners, send_nodes, 0)
    node_in[part] = nodes[part]

    loads[1].wait()
    loads[2].wait()
    loads[3].wait()
    lane_points = lax.broadcasted_iota(jnp.int32, (1, 256), 1)
    first_elem = me * (points // (NP * NP))

    def metric_row(r):
        row = jnp.zeros((1, 256), F32)
        for e in range(points // (NP * NP)):
            row = jnp.where(lane_points >= e * NP * NP, metrics[r, first_elem + e], row)
        return row

    for half in range(2):
        grad = grad_tables[0] * metric_row(2 * half) + grad_tables[1] * metric_row(2 * half + 1)
        high, low = split(grad)
        grad_high[:, half * 256 : half * 256 + 256] = high
        grad_low[:, half * 256 : half * 256 + 256] = low
        vel_xy[0, 0:256, half * 256 : half * 256 + 256] = grad
    padded[128:256, :] = jnp.zeros((128, planes), F32)

    def base_step(c, carry):
        padded[0:points, :] = base_v[c, 0]
        base_t[c] = jnp.transpose(padded[...])
        base_z[c] = dot6(dz[...], base_t[c])
        flow_xy[c] = dot6(base_t[c], vel_xy[0, 0:256, :])
        return carry

    lax.fori_loop(0, 3, base_step, 0)

    rows = pick_table.shape[0]
    point_idx = lax.broadcasted_iota(jnp.int32, (rows, 128), 0)

    def pick_step(j, carry):
        wanted = picks[pl.ds(j, 1), :]
        columns = pl.ds(pl.multiple_of(j * 128, 128), 128)
        pick_table[:, columns] = jnp.where(point_idx == wanted, 1.0, 0.0).astype(BF16)
        return carry

    lax.fori_loop(0, pairs, pick_step, 0)

    def wait_nodes(d, carry):
        origin = part_peer(d)
        part_arrival(node_in.at[origin], node_send, node_recv, origin).wait_recv()
        return carry

    lax.fori_loop(1, partners, wait_nodes, 0)
    lane = lax.broadcasted_iota(jnp.int32, (1, 128), 1)
    left = lane < 64
    node_rows[...] = jnp.zeros((128, 128), F32)
    for j in range(pairs):
        node_rows[j : j + 1, :] = jnp.where(left, node_in[2 * j], node_in[2 * j + 1])
    node_columns = jnp.transpose(node_rows[...])
    node_idx = lax.broadcasted_iota(jnp.int32, (128, NODES_OWN), 1).astype(F32)
    for j in range(pairs):
        node_table[128 * j : 128 * j + 128, :] = jnp.where(
            node_idx == node_columns[:, j : j + 1], 1.0, 0.0
        ).astype(BF16)
    adv_parts[:, rows - 128 : rows] = jnp.zeros((2 * coefs, 128), BF16)

    for load in loads[4:]:
        load.wait()

    def wait_a(d, carry):
        origin = group_peer(d)
        group_arrival(coef_a.at[origin], a_send, a_recv, origin).wait_recv()
        return carry

    lax.fori_loop(1, groups, wait_a, 0)
    high, low = split(coef_a[...].reshape(planes, 256))
    both = dot3(synth_high[...], synth_low[...], high, low)
    vel[0, :, 0:128] = both[0:planes, 0:128]
    vel[1, :, 0:128] = both[0:planes, 128:256]
    along_z[0, :, 0:128] = both[planes : 2 * planes, 0:128]
    along_z[1, :, 0:128] = both[planes : 2 * planes, 128:256]

    def wait_b(d, carry):
        origin = group_peer(d)
        group_arrival(coef_b.at[origin], b_send, b_recv, origin).wait_recv()
        return carry

    lax.fori_loop(1, groups, wait_b, 0)
    high, low = split(coef_b[...].reshape(planes, 256))
    both = dot3(synth_high[...], synth_low[...], high, low)
    vel[2, :, 0:128] = both[0:planes, 0:128]
    along_z[2, :, 0:128] = both[planes : 2 * planes, 0:128]
    for c in range(3):
        rest = both[:, 128:256]
        if c:
            rest = pltpu.roll(rest, 128 - c * extra, 1)
        rest = jnp.where(lane < extra, rest, 0.0)
        vel[c, :, 128:256] = rest[0:planes]
        along_z[c, :, 128:256] = rest[planes : 2 * planes]

    def grad_step(c, carry):
        high, low = split(vel[c])
        vel_xy[c] = dot3(high, low, grad_high[...], grad_low[...])
        return carry

    lax.fori_loop(0, 3, grad_step, 0)

    block = 32
    packed = 24

    for i in range(3):

        def point_step(b, carry, i=i):
            at = pl.ds(pl.multiple_of(b * block, block), block)
            total = jnp.zeros((block, 256), F32)
            for j in range(3):
                slope = along_z[i, at, :] if j == 2 else vel_xy[i, at, j * 256 : j * 256 + 256]
                back = base_z[j, at, :] if i == 2 else flow_xy[j, at, i * 256 : i * 256 + 256]
                total = total - base_t[j, at, :] * slope + vel[j, at, :] * back
            high, low = split(total)
            phys_high[at, :] = high
            phys_low[at, :] = low
            return carry

        lax.fori_loop(0, planes // block, point_step, 0)
        adv[...] = dot3(analysis_high[...], analysis_low[...], phys_high[...], phys_low[...])
        for m in range(groups):
            send_adv[i, m, 0:coefs, :] = adv[m * coefs : (m + 1) * coefs, 0:128]
            rest = adv[m * coefs : (m + 1) * coefs, 128:256]
            second = pltpu.roll(rest[packed : 2 * packed], extra, 1)
            third = pltpu.roll(
                jnp.concatenate([rest[2 * packed :], rest[: 3 * packed - coefs]], axis=0),
                2 * extra,
                1,
            )
            send_adv[i, m, coefs : coefs + packed, :] = jnp.where(
                lane < extra, rest[:packed], jnp.where(lane < 2 * extra, second, third)
            )

        def send_back(d, carry, i=i):
            to = group_peer(d)
            group_copy(
                send_adv.at[i, to], recv_adv.at[i, me], adv_send.at[i], adv_recv.at[i], to, to
            ).start()
            return carry

        lax.fori_loop(1, groups, send_back, 0)
        recv_adv[i, me] = send_adv[i, me]

    stores = []
    for i in range(3):

        def wait_back(d, carry, i=i):
            origin = group_peer(d)
            group_arrival(
                recv_adv.at[i, origin], adv_send.at[i], adv_recv.at[i], origin
            ).wait_recv()
            return carry

        lax.fori_loop(1, groups, wait_back, 0)
        for g in range(groups):
            first = g * points
            rest = recv_adv[i, g, coefs : coefs + packed, :]
            rest = jnp.concatenate(
                [
                    rest,
                    pltpu.roll(rest, 128 - extra, 1),
                    pltpu.roll(rest, 128 - 2 * extra, 1)[: coefs - 2 * packed],
                ],
                axis=0,
            )
            advection[i, :, first : first + 128] = recv_adv[i, g, 0:coefs, :]
            advection[i, :, first + 128 : first + points] = rest[:, :extra]
        store = pltpu.make_async_copy(advection.at[i], advection_hbm.at[i], store_sem.at[i])
        store.start()
        stores.append(store)
        high, low = split(advection[i])
        adv_parts[0:coefs, 0:full] = high
        adv_parts[coefs : 2 * coefs, 0:full] = low
        half = coefs // 2
        wide = min(512, 128 * pairs)
        for tile in range(128 * pairs // wide):
            picked = dot(adv_parts[...], pick_table[:, tile * wide : (tile + 1) * wide])
            picked = picked[0:coefs] + picked[coefs : 2 * coefs]
            for j in range(wide // 128):
                upper = picked[0:half, j * 128 : j * 128 + 128]
                lower = picked[half:coefs, j * 128 : j * 128 + 128]
                owner = 2 * (tile * (wide // 128) + j)
                send_slots[i, owner] = jnp.where(left, upper, pltpu.roll(lower, 64, 1))
                send_slots[i, owner + 1] = jnp.where(left, pltpu.roll(upper, 64, 1), lower)

        def send_picked(d, carry, i=i):
            to = part_peer(d)
            part_copy(
                send_slots.at[i, to], recv_slots.at[i, part], slot_send.at[i], slot_recv.at[i], to
            ).start()
            return carry

        lax.fori_loop(1, partners, send_picked, 0)
        recv_slots[i, part] = send_slots[i, part]

    for i in range(3):

        def wait_picked(d, carry, i=i):
            origin = part_peer(d)
            part_arrival(
                recv_slots.at[i, origin], slot_send.at[i], slot_recv.at[i], origin
            ).wait_recv()
            return carry

        lax.fori_loop(1, partners, wait_picked, 0)
        half = coefs // 2
        for j in range(pairs):
            even = recv_slots[i, 2 * j]
            odd = recv_slots[i, 2 * j + 1]
            upper = jnp.where(left, even, pltpu.roll(odd, 64, 1))
            lower = jnp.where(left, pltpu.roll(even, 64, 1), odd)
            high, low = split(jnp.concatenate([upper, lower], axis=0))
            slot_parts[0:coefs, j * 128 : j * 128 + 128] = high
            slot_parts[coefs : 2 * coefs, j * 128 : j * 128 + 128] = low
        summed = dot(slot_parts[...], node_table[...])
        totals[i] = summed[0:coefs] + summed[coefs : 2 * coefs]
        store = pltpu.make_async_copy(totals.at[i], totals_hbm.at[i], store_sem.at[3 + i])
        store.start()
        stores.append(store)

    def sent_group(d, carry):
        to = group_peer(d)
        group_copy(stage_a.at[to], coef_a.at[me], a_send, a_recv, to, to).wait_send()
        group_copy(stage_b.at[to], coef_b.at[me], b_send, b_recv, to, to).wait_send()
        for i in range(3):
            group_copy(
                send_adv.at[i, to], recv_adv.at[i, me], adv_send.at[i], adv_recv.at[i], to, to
            ).wait_send()
        return carry

    lax.fori_loop(1, groups, sent_group, 0)

    def sent_part(d, carry):
        to = part_peer(d)
        part_copy(nodes.at[to], node_in.at[part], node_send, node_recv, to).wait_send()
        for i in range(3):
            part_copy(
                send_slots.at[i, to], recv_slots.at[i, part], slot_send.at[i], slot_recv.at[i], to
            ).wait_send()
        return carry

    lax.fori_loop(1, partners, sent_part, 0)
    for store in stores:
        store.wait()


def per_device(adjoint_modes, base_planes, metrics, send_point, dest_node, pair_counts):
    components, coefs, local_points = adjoint_modes.shape
    planes = base_planes.shape[3]
    groups = lax.axis_size("modes")
    partners = lax.axis_size("elems")
    points = local_points // groups
    pairs = partners // 2
    slot_count = send_point.shape[2]
    synth, analysis, slope, dz = spectral_tables(planes)
    synth_high, synth_low = halves_of(np.concatenate([synth, slope], axis=0))
    analysis_high, analysis_low = halves_of(analysis)
    grad = gradient_tables(points // (NP * NP), 256)

    live = jnp.arange(slot_count, dtype=jnp.int32)[None, :] < pair_counts[0][:, None]
    picks = jnp.where(live, send_point[0], -1).reshape(pairs, 2 * slot_count)
    nodes = jnp.where(live, dest_node[0], -1).astype(F32)
    nodes = jnp.concatenate([nodes, nodes], axis=1)[:, None, :]

    rows = -(-local_points // 128) * 128
    any_spec = pl.BlockSpec(memory_space=pl.ANY)
    vmem_spec = pl.BlockSpec(memory_space=pltpu.VMEM)
    smem_spec = pl.BlockSpec(memory_space=pltpu.SMEM)

    def room(*shape, dtype=F32):
        return pltpu.VMEM(shape, dtype)

    dma = pltpu.SemaphoreType.DMA
    scratch = [
        room(3, coefs, local_points),
        room(3, 1, points, planes),
        room(2 * planes, planes, dtype=BF16),
        room(2 * planes, planes, dtype=BF16),
        room(planes, planes),
        room(planes, planes, dtype=BF16),
        room(planes, planes, dtype=BF16),
        room(2, 256, 256),
        room(groups, coefs, 256),
        room(groups, coefs, 256),
        room(groups, coefs, 256),
        room(groups, coefs, 256),
        room(256, planes),
        room(3, planes, 256),
        room(3, planes, 256),
        room(3, planes, 512),
        room(256, 512, dtype=BF16),
        room(256, 512, dtype=BF16),
        room(rows, pairs * 128, dtype=BF16),
        room(128, 128),
        room(pairs * 128, NODES_OWN, dtype=BF16),
        room(partners, 1, 128),
        room(3, planes, 256),
        room(3, planes, 256),
        room(3, planes, 512),
        room(planes, 256, dtype=BF16),
        room(planes, 256, dtype=BF16),
        room(planes, 256),
        room(3, groups, coefs + 24, 128),
        room(3, groups, coefs + 24, 128),
        room(3, coefs, local_points),
        room(2 * coefs, rows, dtype=BF16),
        room(3, partners, coefs // 2, 128),
        room(3, partners, coefs // 2, 128),
        room(2 * coefs, pairs * 128, dtype=BF16),
        room(3, coefs, NODES_OWN),
        dma((8,)),
        dma((6,)),
        dma((groups,)),
        dma((groups,)),
        dma((groups,)),
        dma((groups,)),
        dma((3, groups)),
        dma((3, groups)),
        dma((partners,)),
        dma((partners,)),
        dma((3, partners)),
        dma((3, partners)),
    ]

    def kernel(*refs):
        body(groups, partners, points, *refs)

    return pl.pallas_call(
        kernel,
        out_shape=(
            jax.ShapeDtypeStruct((3, coefs, local_points), F32),
            jax.ShapeDtypeStruct((3, coefs, NODES_OWN), F32),
        ),
        in_specs=[any_spec, any_spec, smem_spec, vmem_spec, vmem_spec] + [any_spec] * 6,
        out_specs=(any_spec, any_spec),
        scratch_shapes=scratch,
        compiler_params=pltpu.CompilerParams(
            collective_id=0, has_side_effects=True, vmem_limit_bytes=56 * 1024 * 1024
        ),
    )(
        adjoint_modes,
        base_planes,
        metrics,
        picks,
        nodes,
        synth_high,
        synth_low,
        jnp.asarray(dz, dtype=F32),
        analysis_high,
        analysis_low,
        grad,
    )


def solution(mesh):
    return jax.shard_map(
        per_device,
        mesh=mesh,
        in_specs=(
            P(None, "modes", "elems"),
            P(None, "modes", "elems", None),
            P(None, "elems"),
            P("elems", None, None),
            P("elems", None, None),
            P("elems", None),
        ),
        out_specs=(P(None, "modes", "elems"), P(None, "modes", "elems")),
        check_vma=False,
    )
```

```python
import jax
import jax.numpy as jnp
import numpy as np
from jax import lax
from jax.experimental import pallas as pl
from jax.experimental.pallas import tpu as pltpu
from jax.sharding import PartitionSpec as P

NP = 9
NODES_OWN = 512
MESH = pl.DeviceIdType.MESH
F32 = jnp.float32
BF16 = jnp.bfloat16

span_wavenumber = 0.4

CHUNKS = ((0, 0, 16, 2), (0, 16, 48, 3), (1, 0, 64, 3), (2, 0, 64, 3))


def packed_rows(count, fold):
    return -(-count // (8 * fold)) * 8


def chebyshev_table(count):
    degree = count - 1
    position = np.arange(count)
    node_x = np.cos(np.pi * position / degree)
    weights = np.where((position == 0) | (position == degree), 2.0, 1.0)
    sign_terms = (-1.0) ** position
    identity = np.eye(count)
    spacing = node_x[:, None] - node_x[None, :] + identity
    matrix = (
        weights[:, None] * sign_terms[:, None] / (weights[None, :] * sign_terms[None, :]) / spacing
    )
    matrix = matrix * (1.0 - identity)
    matrix = matrix - identity * matrix.sum(axis=1)[:, None]
    return matrix


def spectral_tables(planes):
    position = np.arange(planes)
    wavenumber = np.where(position == 1, planes // 2, position // 2)
    angles = 2.0 * np.pi / planes * (position[:, None] * wavenumber[None, :] % planes)
    sine_col = (position % 2 == 1) & (position != 1)
    synth_table = np.where(sine_col[None, :], np.sin(angles), np.cos(angles))
    weighting = np.where(position <= 1, 1.0, 2.0) / planes
    analysis = synth_table.T * weighting[:, None]
    speeds = span_wavenumber * wavenumber
    slope_table = np.where(
        position[None, :] <= 1,
        0.0,
        np.where(
            sine_col[None, :], speeds[None, :] * np.cos(angles), -speeds[None, :] * np.sin(angles)
        ),
    )
    return synth_table, analysis, slope_table, slope_table @ analysis


def halves_of(table):
    single = table.astype(np.float32)
    high = single.astype(BF16)
    low = (single - high.astype(np.float32)).astype(BF16)
    return high, low


def gradient_tables(sub_elems, width):
    diff = chebyshev_table(NP)
    points = sub_elems * NP * NP
    tables = np.zeros((2, width, width), np.float32)
    along = (np.kron(diff, np.eye(NP)), np.kron(np.eye(NP), diff))
    for direction in range(2):
        for elem in range(sub_elems):
            rows = slice(elem * NP * NP, (elem + 1) * NP * NP)
            tables[direction, rows, rows] = along[direction].T
    assert points <= width
    return tables


def split(value):
    high = value.astype(BF16)
    return high, (value - high.astype(F32)).astype(BF16)


def dot(left, right):
    return jnp.dot(left, right, preferred_element_type=F32)


def dot3(left_high, left_low, right_high, right_low):
    return dot(left_high, right_high) + (dot(left_high, right_low) + dot(left_low, right_high))


def dot6(left, right):
    return jnp.dot(left, right, precision=lax.Precision.HIGHEST, preferred_element_type=F32)


def body(
    groups,
    partners,
    points,
    x_hbm,
    base_hbm,
    metrics_hbm,
    send_point_hbm,
    dest_node_hbm,
    pair_counts_hbm,
    synth_high_hbm,
    synth_low_hbm,
    dz_hbm,
    analysis_high_hbm,
    analysis_low_hbm,
    grad_hbm,
    advection_hbm,
    totals_hbm,
    x_v,
    base_v,
    metrics,
    send_point,
    dest_node,
    pair_counts,
    synth_high,
    synth_low,
    dz,
    analysis_high,
    analysis_low,
    grad_tables,
    stage_a,
    stage_b,
    coef_a,
    coef_b,
    padded,
    base_t,
    base_z,
    flow_xy,
    grad_high,
    grad_low,
    picks,
    nodes,
    pick_table,
    node_rows,
    node_table,
    node_in,
    vel,
    along_z,
    vel_xy,
    phys_high,
    phys_low,
    adv,
    advection,
    adv_parts,
    slot_parts,
    totals,
    load_sem,
    store_sem,
    a_send,
    a_recv,
    b_send,
    b_recv,
    adv_send,
    adv_recv,
    node_send,
    node_recv,
    slot_send,
    slot_recv,
    *chunk_rooms,
):
    send_adv, recv_adv, send_slots, recv_slots = (
        chunk_rooms[i * len(CHUNKS) : (i + 1) * len(CHUNKS)] for i in range(4)
    )
    me = lax.axis_index("modes")
    part = lax.axis_index("elems")
    planes = dz.shape[0]
    coefs = planes // groups
    extra = points - 128
    pairs = partners // 2
    full = groups * points

    barrier = pltpu.get_barrier_semaphore()

    def group_peer(d):
        return lax.rem(me + d, groups)

    def part_peer(d):
        return lax.rem(part + d, partners)

    def greet_group(d, carry):
        pl.semaphore_signal(barrier, inc=1, device_id=(group_peer(d), part), device_id_type=MESH)
        return carry

    def greet_part(d, carry):
        pl.semaphore_signal(barrier, inc=1, device_id=(me, part_peer(d)), device_id_type=MESH)
        return carry

    lax.fori_loop(1, groups, greet_group, 0)
    lax.fori_loop(1, partners, greet_part, 0)

    loads = [
        pltpu.make_async_copy(source, target, load_sem.at[i])
        for i, (source, target) in enumerate(
            (
                (x_hbm, x_v),
                (send_point_hbm, send_point),
                (dest_node_hbm, dest_node),
                (pair_counts_hbm, pair_counts),
                (metrics_hbm, metrics),
                (base_hbm, base_v),
                (grad_hbm, grad_tables),
                (dz_hbm, dz),
                (synth_high_hbm, synth_high),
                (synth_low_hbm, synth_low),
                (analysis_high_hbm, analysis_high),
                (analysis_low_hbm, analysis_low),
            )
        )
    ]
    for load in loads:
        load.start()

    loads[0].wait()
    for g in range(groups):
        first = g * points
        stage_a[g, :, 0:128] = x_v[0, :, first : first + 128]
        stage_a[g, :, 128:256] = x_v[1, :, first : first + 128]
        stage_b[g, :, 0:128] = x_v[2, :, first : first + 128]
        rest = [x_v[c, :, first + 128 : first + points] for c in range(3)]
        rest.append(jnp.zeros((coefs, 128 - 3 * extra), F32))
        stage_b[g, :, 128:256] = jnp.concatenate(rest, axis=1)

    pl.semaphore_wait(barrier, groups - 1 + partners - 1)

    def group_copy(source, target, send, recv, to, slot):
        return pltpu.make_async_remote_copy(
            src_ref=source,
            dst_ref=target,
            send_sem=send.at[slot],
            recv_sem=recv.at[me],
            device_id=(to, part),
            device_id_type=MESH,
        )

    def group_arrival(target, send, recv, origin):
        return pltpu.make_async_remote_copy(
            src_ref=target,
            dst_ref=target,
            send_sem=send.at[origin],
            recv_sem=recv.at[origin],
            device_id=(origin, part),
            device_id_type=MESH,
        )

    def send_a(d, carry):
        to = group_peer(d)
        group_copy(stage_a.at[to], coef_a.at[me], a_send, a_recv, to, to).start()
        return carry

    def send_b(d, carry):
        to = group_peer(d)
        group_copy(stage_b.at[to], coef_b.at[me], b_send, b_recv, to, to).start()
        return carry

    lax.fori_loop(1, groups, send_a, 0)
    lax.fori_loop(1, groups, send_b, 0)
    coef_a[me] = stage_a[me]
    coef_b[me] = stage_b[me]

    for load in loads[1:4]:
        load.wait()
    owner_idx = lax.broadcasted_iota(jnp.int32, (partners, 64), 0)
    slot_idx = lax.broadcasted_iota(jnp.int32, (partners, 64), 1)
    live = jnp.zeros((partners, 64), jnp.int32)
    for o in range(partners):
        live = jnp.where(owner_idx == o, pair_counts[0, o], live)
    live = slot_idx < live
    wanted = jnp.where(live, send_point[0], -1)
    fed = jnp.where(live, dest_node[0], -1).astype(F32)
    for o in range(partners):
        side = o % 2 * 64
        picks[o // 2 : o // 2 + 1, side : side + 64] = wanted[o : o + 1]
        nodes[o, :, 0:64] = fed[o : o + 1]
        nodes[o, :, 64:128] = fed[o : o + 1]

    def part_copy(source, target, send, recv, to):
        return pltpu.make_async_remote_copy(
            src_ref=source,
            dst_ref=target,
            send_sem=send.at[to],
            recv_sem=recv.at[part],
            device_id=(me, to),
            device_id_type=MESH,
        )

    def part_arrival(target, send, recv, origin):
        return pltpu.make_async_remote_copy(
            src_ref=target,
            dst_ref=target,
            send_sem=send.at[origin],
            recv_sem=recv.at[origin],
            device_id=(me, origin),
            device_id_type=MESH,
        )

    def send_nodes(d, carry):
        to = part_peer(d)
        part_copy(nodes.at[to], node_in.at[part], node_send, node_recv, to).start()
        return carry

    lax.fori_loop(1, partners, send_nodes, 0)
    node_in[part] = nodes[part]

    for load in loads[4:8]:
        load.wait()
    lane_points = lax.broadcasted_iota(jnp.int32, (1, 256), 1)
    first_elem = me * (points // (NP * NP))

    def metric_row(r):
        row = jnp.zeros((1, 256), F32)
        for e in range(points // (NP * NP)):
            row = jnp.where(lane_points >= e * NP * NP, metrics[r, first_elem + e], row)
        return row

    for half in range(2):
        grad = grad_tables[0] * metric_row(2 * half) + grad_tables[1] * metric_row(2 * half + 1)
        high, low = split(grad)
        grad_high[:, half * 256 : half * 256 + 256] = high
        grad_low[:, half * 256 : half * 256 + 256] = low
        vel_xy[0:256, half * 256 : half * 256 + 256] = grad
    padded[128:256, :] = jnp.zeros((128, planes), F32)

    def base_step(c, carry):
        padded[0:points, :] = base_v[c, :, 0, :]
        base_t[c] = jnp.transpose(padded[...])
        base_z[c] = dot6(dz[...], base_t[c])
        flow_xy[c] = dot6(base_t[c], vel_xy[0:256, :])
        return carry

    lax.fori_loop(0, 3, base_step, 0)

    rows = pick_table.shape[0]
    point_idx = lax.broadcasted_iota(jnp.int32, (rows, 128), 0)

    def pick_step(j, carry):
        wanted = picks[pl.ds(j, 1), :]
        columns = pl.ds(pl.multiple_of(j * 128, 128), 128)
        pick_table[:, columns] = jnp.where(point_idx == wanted, 1.0, 0.0).astype(BF16)
        return carry

    lax.fori_loop(0, pairs, pick_step, 0)

    def wait_nodes(d, carry):
        origin = part_peer(d)
        part_arrival(node_in.at[origin], node_send, node_recv, origin).wait_recv()
        return carry

    lax.fori_loop(1, partners, wait_nodes, 0)
    lane = lax.broadcasted_iota(jnp.int32, (1, 128), 1)
    left = lane < 64
    node_rows[...] = jnp.zeros((128, 128), F32)
    for j in range(pairs):
        node_rows[j : j + 1, :] = jnp.where(left, node_in[2 * j], node_in[2 * j + 1])
    node_columns = jnp.transpose(node_rows[...])
    node_idx = lax.broadcasted_iota(jnp.int32, (128, NODES_OWN), 1).astype(F32)
    for j in range(pairs):
        node_table[128 * j : 128 * j + 128, :] = jnp.where(
            node_idx == node_columns[:, j : j + 1], 1.0, 0.0
        ).astype(BF16)
    adv_parts[:, rows - 128 : rows] = jnp.zeros((2 * coefs, 128), BF16)

    for load in loads[8:]:
        load.wait()

    def wait_a(d, carry):
        origin = group_peer(d)
        group_arrival(coef_a.at[origin], a_send, a_recv, origin).wait_recv()
        return carry

    lax.fori_loop(1, groups, wait_a, 0)
    high, low = split(coef_a[...].reshape(planes, 256))
    both = dot3(synth_high[...], synth_low[...], high, low)
    vel[0, :, 0:128] = both[0:planes, 0:128]
    vel[1, :, 0:128] = both[0:planes, 128:256]
    along_z[0, :, 0:128] = both[planes : 2 * planes, 0:128]
    along_z[1, :, 0:128] = both[planes : 2 * planes, 128:256]

    def wait_b(d, carry):
        origin = group_peer(d)
        group_arrival(coef_b.at[origin], b_send, b_recv, origin).wait_recv()
        return carry

    lax.fori_loop(1, groups, wait_b, 0)
    high, low = split(coef_b[...].reshape(planes, 256))
    both = dot3(synth_high[...], synth_low[...], high, low)
    vel[2, :, 0:128] = both[0:planes, 0:128]
    along_z[2, :, 0:128] = both[planes : 2 * planes, 0:128]
    for c in range(3):
        rest = both[:, 128:256]
        if c:
            rest = pltpu.roll(rest, 128 - c * extra, 1)
        rest = jnp.where(lane < extra, rest, 0.0)
        vel[c, :, 128:256] = rest[0:planes]
        along_z[c, :, 128:256] = rest[planes : 2 * planes]

    block = 32

    def advect(i):
        high, low = split(vel[i])
        vel_xy[...] = dot3(high, low, grad_high[...], grad_low[...])

        def point_step(b, carry):
            at = pl.ds(pl.multiple_of(b * block, block), block)
            total = jnp.zeros((block, 256), F32)
            for j in range(3):
                slope = along_z[i, at, :] if j == 2 else vel_xy[at, j * 256 : j * 256 + 256]
                back = base_z[j, at, :] if i == 2 else flow_xy[j, at, i * 256 : i * 256 + 256]
                total = total - base_t[j, at, :] * slope + vel[j, at, :] * back
            high, low = split(total)
            phys_high[at, :] = high
            phys_low[at, :] = low
            return carry

        lax.fori_loop(0, planes // block, point_step, 0)
        adv[...] = dot3(analysis_high[...], analysis_low[...], phys_high[...], phys_low[...])

    def back_copy(n, to):
        return group_copy(
            send_adv[n].at[to], recv_adv[n].at[me], adv_send.at[n], adv_recv.at[n], to, to
        )

    def send_back(n):
        _, start, count, fold = CHUNKS[n]
        packed = packed_rows(count, fold)
        for m in range(groups):
            at = m * coefs + start
            send_adv[n][m, 0:count, :] = adv[at : at + count, 0:128]
            rest = adv[at : at + count, 128:256]
            merged = rest[:packed]
            for f in range(1, fold):
                piece = rest[f * packed : min((f + 1) * packed, count)]
                if piece.shape[0] < packed:
                    filler = jnp.zeros((packed - piece.shape[0], 128), F32)
                    piece = jnp.concatenate([piece, filler], axis=0)
                merged = jnp.where(lane < f * extra, merged, pltpu.roll(piece, f * extra, 1))
            send_adv[n][m, count : count + packed, :] = merged

        def step(d, carry):
            back_copy(n, group_peer(d)).start()
            return carry

        lax.fori_loop(1, groups, step, 0)
        recv_adv[n][me] = send_adv[n][me]

    stores = []

    def slot_copy(n, to):
        return part_copy(
            send_slots[n].at[to], recv_slots[n].at[part], slot_send.at[n], slot_recv.at[n], to
        )

    wide = min(512, 128 * pairs)
    tiles = 128 * pairs // wide
    tile_owners = 2 * (wide // 128)

    def send_picked(n):
        i, start, count, fold = CHUNKS[n]
        packed = packed_rows(count, fold)

        def arrive(d, carry):
            origin = group_peer(d)
            group_arrival(
                recv_adv[n].at[origin], adv_send.at[n], adv_recv.at[n], origin
            ).wait_recv()
            return carry

        lax.fori_loop(1, groups, arrive, 0)
        for g in range(groups):
            first = g * points
            rest = recv_adv[n][g, count : count + packed, :]
            pieces = [rest]
            for f in range(1, fold):
                piece = pltpu.roll(rest, 128 - f * extra, 1)
                pieces.append(piece[: min(packed, count - f * packed)])
            rest = jnp.concatenate(pieces, axis=0)
            advection[i, start : start + count, first : first + 128] = recv_adv[n][g, 0:count, :]
            advection[i, start : start + count, first + 128 : first + points] = rest[:, :extra]
        store = pltpu.make_async_copy(
            advection.at[i, pl.ds(start, count)],
            advection_hbm.at[i, pl.ds(start, count)],
            store_sem.at[n],
        )
        store.start()
        stores.append(store)
        high, low = split(advection[i, start : start + count, :])
        adv_parts[0:count, 0:full] = high
        adv_parts[count : 2 * count, 0:full] = low
        half = count // 2

        def pick(t, carry):
            tile = lax.rem(part // tile_owners + t, tiles)
            columns = pl.ds(pl.multiple_of(tile * wide, 128), wide)
            picked = dot(adv_parts[0 : 2 * count, :], pick_table[:, columns])
            picked = picked[0:count] + picked[count : 2 * count]
            for j in range(wide // 128):
                upper = picked[0:half, j * 128 : j * 128 + 128]
                lower = picked[half:count, j * 128 : j * 128 + 128]
                owner = tile * tile_owners + 2 * j
                send_slots[n][owner] = jnp.where(left, upper, pltpu.roll(lower, 64, 1))
                send_slots[n][owner + 1] = jnp.where(left, pltpu.roll(upper, 64, 1), lower)

            def step(q, carry):
                to = tile * tile_owners + q

                @pl.when(to != part)
                def _():
                    slot_copy(n, to).start()

                return carry

            return lax.fori_loop(0, tile_owners, step, carry)

        lax.fori_loop(0, tiles, pick, 0)
        recv_slots[n][part] = send_slots[n][part]

    def add_nodes(n):
        i, start, count, _ = CHUNKS[n]

        def arrive(d, carry):
            origin = part_peer(d)
            part_arrival(
                recv_slots[n].at[origin], slot_send.at[n], slot_recv.at[n], origin
            ).wait_recv()
            return carry

        lax.fori_loop(1, partners, arrive, 0)
        for j in range(pairs):
            even = recv_slots[n][2 * j]
            odd = recv_slots[n][2 * j + 1]
            upper = jnp.where(left, even, pltpu.roll(odd, 64, 1))
            lower = jnp.where(left, pltpu.roll(even, 64, 1), odd)
            high, low = split(jnp.concatenate([upper, lower], axis=0))
            slot_parts[0:count, j * 128 : j * 128 + 128] = high
            slot_parts[count : 2 * count, j * 128 : j * 128 + 128] = low
        summed = dot(slot_parts[0 : 2 * count, :], node_table[...])
        totals[i, start : start + count, :] = summed[0:count] + summed[count : 2 * count]
        store = pltpu.make_async_copy(
            totals.at[i, pl.ds(start, count)],
            totals_hbm.at[i, pl.ds(start, count)],
            store_sem.at[len(CHUNKS) + n],
        )
        store.start()
        stores.append(store)

    advect(0)
    send_back(0)
    send_back(1)
    advect(1)
    send_back(2)
    send_picked(0)
    send_picked(1)
    advect(2)
    for n in range(3, len(CHUNKS)):
        send_back(n)
    for n in range(2, len(CHUNKS)):
        send_picked(n)
    for n in range(len(CHUNKS)):
        add_nodes(n)

    def sent_group(d, carry):
        to = group_peer(d)
        group_copy(stage_a.at[to], coef_a.at[me], a_send, a_recv, to, to).wait_send()
        group_copy(stage_b.at[to], coef_b.at[me], b_send, b_recv, to, to).wait_send()
        for n in range(len(CHUNKS)):
            back_copy(n, to).wait_send()
        return carry

    lax.fori_loop(1, groups, sent_group, 0)

    def sent_part(d, carry):
        to = part_peer(d)
        part_copy(nodes.at[to], node_in.at[part], node_send, node_recv, to).wait_send()
        for n in range(len(CHUNKS)):
            slot_copy(n, to).wait_send()
        return carry

    lax.fori_loop(1, partners, sent_part, 0)
    for store in stores:
        store.wait()


def per_device(adjoint_modes, base_planes, metrics, send_point, dest_node, pair_counts):
    components, coefs, local_points = adjoint_modes.shape
    planes = base_planes.shape[3]
    groups = lax.axis_size("modes")
    partners = lax.axis_size("elems")
    points = local_points // groups
    pairs = partners // 2
    synth, analysis, slope, dz = spectral_tables(planes)
    synth_high, synth_low = halves_of(np.concatenate([synth, slope], axis=0))
    analysis_high, analysis_low = halves_of(analysis)
    grad = gradient_tables(points // (NP * NP), 256)

    rows = -(-local_points // 128) * 128
    any_spec = pl.BlockSpec(memory_space=pl.ANY)

    def room(*shape, dtype=F32):
        return pltpu.VMEM(shape, dtype)

    dma = pltpu.SemaphoreType.DMA
    scratch = [
        room(3, coefs, local_points),
        room(3, points, 1, planes),
        pltpu.SMEM(metrics.shape, F32),
        room(*send_point.shape, dtype=jnp.int32),
        room(*dest_node.shape, dtype=jnp.int32),
        pltpu.SMEM(pair_counts.shape, jnp.int32),
        room(2 * planes, planes, dtype=BF16),
        room(2 * planes, planes, dtype=BF16),
        room(planes, planes),
        room(planes, planes, dtype=BF16),
        room(planes, planes, dtype=BF16),
        room(2, 256, 256),
        room(groups, coefs, 256),
        room(groups, coefs, 256),
        room(groups, coefs, 256),
        room(groups, coefs, 256),
        room(256, planes),
        room(3, planes, 256),
        room(3, planes, 256),
        room(3, planes, 512),
        room(256, 512, dtype=BF16),
        room(256, 512, dtype=BF16),
        room(pairs, 128, dtype=jnp.int32),
        room(partners, 1, 128),
        room(rows, pairs * 128, dtype=BF16),
        room(128, 128),
        room(pairs * 128, NODES_OWN, dtype=BF16),
        room(partners, 1, 128),
        room(3, planes, 256),
        room(3, planes, 256),
        room(planes, 512),
        room(planes, 256, dtype=BF16),
        room(planes, 256, dtype=BF16),
        room(planes, 256),
        room(3, coefs, local_points),
        room(2 * coefs, rows, dtype=BF16),
        room(2 * coefs, pairs * 128, dtype=BF16),
        room(3, coefs, NODES_OWN),
        dma((12,)),
        dma((2 * len(CHUNKS),)),
        dma((groups,)),
        dma((groups,)),
        dma((groups,)),
        dma((groups,)),
        dma((len(CHUNKS), groups)),
        dma((len(CHUNKS), groups)),
        dma((partners,)),
        dma((partners,)),
        dma((len(CHUNKS), partners)),
        dma((len(CHUNKS), partners)),
    ]
    for _ in range(2):
        for _, _, count, fold in CHUNKS:
            scratch.append(room(groups, count + packed_rows(count, fold), 128))
    for _ in range(2):
        for _, _, count, _ in CHUNKS:
            scratch.append(room(partners, count // 2, 128))

    def kernel(*refs):
        body(groups, partners, points, *refs)

    results = pl.pallas_call(
        kernel,
        out_shape=(
            jax.ShapeDtypeStruct((3, coefs, local_points), F32),
            jax.ShapeDtypeStruct((3, coefs, NODES_OWN), F32),
        ),
        in_specs=[any_spec] * 12,
        out_specs=(any_spec, any_spec),
        scratch_shapes=scratch,
        compiler_params=pltpu.CompilerParams(
            collective_id=0, has_side_effects=True, vmem_limit_bytes=56 * 1024 * 1024
        ),
    )(
        adjoint_modes,
        jnp.transpose(base_planes, (0, 2, 1, 3)),
        metrics,
        send_point,
        dest_node,
        pair_counts,
        synth_high,
        synth_low,
        jnp.asarray(dz, dtype=F32),
        analysis_high,
        analysis_low,
        grad,
    )

    def hand_over(advection, totals, advection_out, totals_out, held, held_totals, sem_in, sem_out):
        pieces = [
            (advection.at[c], held.at[c], advection_out.at[c]) for c in range(components)
        ] + [(totals, held_totals, totals_out)]
        loads = [
            pltpu.make_async_copy(source, middle, sem_in.at[i])
            for i, (source, middle, _) in enumerate(pieces)
        ]
        stores = [
            pltpu.make_async_copy(middle, target, sem_out.at[i])
            for i, (_, middle, target) in enumerate(pieces)
        ]
        for load in loads:
            load.start()
        for load, store in zip(loads, stores):
            load.wait()
            store.start()
        for store in stores:
            store.wait()

    return pl.pallas_call(
        hand_over,
        out_shape=tuple(jax.ShapeDtypeStruct(r.shape, r.dtype) for r in results),
        in_specs=[any_spec, any_spec],
        out_specs=(any_spec, any_spec),
        scratch_shapes=[room(*r.shape) for r in results] + [dma((components + 1,))] * 2,
        compiler_params=pltpu.CompilerParams(vmem_limit_bytes=56 * 1024 * 1024),
    )(*results)


def solution(mesh):
    return jax.shard_map(
        per_device,
        mesh=mesh,
        in_specs=(
            P(None, "modes", "elems"),
            P(None, "modes", "elems", None),
            P(None, "elems"),
            P("elems", None, None),
            P("elems", None, None),
            P("elems", None),
        ),
        out_specs=(P(None, "modes", "elems"), P(None, "modes", "elems")),
        check_vma=False,
    )
```

```python
import jax
import jax.numpy as jnp
import numpy as np
from jax import lax
from jax.experimental import pallas as pl
from jax.experimental.pallas import tpu as pltpu
from jax.sharding import PartitionSpec as P

NP = 9
NODES_OWN = 512
MESH = pl.DeviceIdType.MESH
F32 = jnp.float32
BF16 = jnp.bfloat16

span_wavenumber = 0.4

CHUNKS = ((0, 0, 64, 3, 16), (1, 0, 64, 3, 16), (2, 0, 64, 3, 16))

RING = 8
UP, DOWN, HERE = 0, 1, 2
DISTANCES = (4, 3, 5, 2, 6, 1, 7, 0)


def routes(distance):
    if distance == 0:
        return ((HERE, 0),)
    if 2 * distance == RING:
        return ((UP, distance - 1), (DOWN, distance - 1))
    if 2 * distance < RING:
        return ((UP, distance - 1),)
    return ((DOWN, RING - distance - 1),)


def packed_rows(count, fold):
    return -(-count // (8 * fold)) * 8


def chebyshev_table(count):
    degree = count - 1
    position = np.arange(count)
    node_x = np.cos(np.pi * position / degree)
    weights = np.where((position == 0) | (position == degree), 2.0, 1.0)
    sign_terms = (-1.0) ** position
    identity = np.eye(count)
    spacing = node_x[:, None] - node_x[None, :] + identity
    matrix = (
        weights[:, None] * sign_terms[:, None] / (weights[None, :] * sign_terms[None, :]) / spacing
    )
    matrix = matrix * (1.0 - identity)
    matrix = matrix - identity * matrix.sum(axis=1)[:, None]
    return matrix


def spectral_tables(planes):
    position = np.arange(planes)
    wavenumber = np.where(position == 1, planes // 2, position // 2)
    angles = 2.0 * np.pi / planes * (position[:, None] * wavenumber[None, :] % planes)
    sine_col = (position % 2 == 1) & (position != 1)
    synth_table = np.where(sine_col[None, :], np.sin(angles), np.cos(angles))
    weighting = np.where(position <= 1, 1.0, 2.0) / planes
    analysis = synth_table.T * weighting[:, None]
    speeds = span_wavenumber * wavenumber
    slope_table = np.where(
        position[None, :] <= 1,
        0.0,
        np.where(
            sine_col[None, :], speeds[None, :] * np.cos(angles), -speeds[None, :] * np.sin(angles)
        ),
    )
    return synth_table, analysis, slope_table, slope_table @ analysis


def halves_of(table):
    single = table.astype(np.float32)
    high = single.astype(BF16)
    low = (single - high.astype(np.float32)).astype(BF16)
    return high, low


def gradient_tables(sub_elems, width):
    diff = chebyshev_table(NP)
    points = sub_elems * NP * NP
    tables = np.zeros((2, width, width), np.float32)
    along = (np.kron(diff, np.eye(NP)), np.kron(np.eye(NP), diff))
    for direction in range(2):
        for elem in range(sub_elems):
            rows = slice(elem * NP * NP, (elem + 1) * NP * NP)
            tables[direction, rows, rows] = along[direction].T
    assert points <= width
    return tables


def split(value):
    high = value.astype(BF16)
    return high, (value - high.astype(F32)).astype(BF16)


def dot(left, right):
    return jnp.dot(left, right, preferred_element_type=F32)


def dot3(left_high, left_low, right_high, right_low):
    return dot(left_high, right_high) + (dot(left_high, right_low) + dot(left_low, right_high))


def dot6(left, right):
    return jnp.dot(left, right, precision=lax.Precision.HIGHEST, preferred_element_type=F32)


def body(
    groups,
    partners,
    points,
    x_hbm,
    base_hbm,
    metrics_hbm,
    send_point_hbm,
    dest_node_hbm,
    pair_counts_hbm,
    synth_high_hbm,
    synth_low_hbm,
    dz_hbm,
    analysis_high_hbm,
    analysis_low_hbm,
    grad_hbm,
    advection_hbm,
    totals_hbm,
    x_v,
    base_v,
    metrics,
    send_point,
    dest_node,
    pair_counts,
    synth_high,
    synth_low,
    dz,
    analysis_high,
    analysis_low,
    grad_tables,
    stage_a,
    stage_b,
    coef_a,
    coef_b,
    padded,
    base_t,
    base_z,
    flow_xy,
    grad_high,
    grad_low,
    picks,
    nodes,
    pick_table,
    node_rows,
    node_table,
    node_in,
    vel,
    along_z,
    vel_xy,
    phys_high,
    phys_low,
    adv,
    advection,
    adv_parts,
    slot_parts,
    totals,
    dense,
    dense_in,
    load_sem,
    store_sem,
    a_send,
    a_recv,
    b_send,
    b_recv,
    adv_send,
    adv_recv,
    node_send,
    node_recv,
    slot_send,
    slot_recv,
    dense_send,
    dense_recv,
    *chunk_rooms,
):
    send_adv, recv_adv, send_slots, recv_slots = (
        chunk_rooms[i * len(CHUNKS) : (i + 1) * len(CHUNKS)] for i in range(4)
    )
    me = lax.axis_index("modes")
    part = lax.axis_index("elems")
    planes = dz.shape[0]
    coefs = planes // groups
    extra = points - 128
    pairs = partners // 2
    full = groups * points
    side = partners // RING
    level = part // side
    column = lax.rem(part, side)
    reach = RING // 2
    blocks = 2 * reach * side + side

    def device_at(steps, other):
        return lax.rem(level + steps + RING, RING) * side + other

    def block_at(way, steps, other):
        return (way * reach + steps) * side + other

    barrier = pltpu.get_barrier_semaphore()

    def group_peer(d):
        return lax.rem(me + d, groups)

    def greet_group(d, carry):
        pl.semaphore_signal(barrier, inc=1, device_id=(group_peer(d), part), device_id_type=MESH)
        return carry

    def greet_part(d, carry):
        to = device_at(d // side - reach + 1, lax.rem(d, side))

        @pl.when(to != part)
        def _():
            pl.semaphore_signal(barrier, inc=1, device_id=(me, to), device_id_type=MESH)

        return carry

    lax.fori_loop(1, groups, greet_group, 0)
    lax.fori_loop(0, (2 * reach - 1) * side, greet_part, 0)

    loads = [
        pltpu.make_async_copy(source, target, load_sem.at[i])
        for i, (source, target) in enumerate(
            (
                (x_hbm, x_v),
                (send_point_hbm, send_point),
                (dest_node_hbm, dest_node),
                (pair_counts_hbm, pair_counts),
                (metrics_hbm, metrics),
                (base_hbm, base_v),
                (grad_hbm, grad_tables),
                (dz_hbm, dz),
                (synth_high_hbm, synth_high),
                (synth_low_hbm, synth_low),
                (analysis_high_hbm, analysis_high),
                (analysis_low_hbm, analysis_low),
            )
        )
    ]
    loads[0].start()

    for n, (_, _, count, _, upward) in enumerate(CHUNKS):
        for other in range(side):
            if upward < count // 2:
                recv_slots[n][block_at(UP, reach - 1, other), upward : count // 2, :] = jnp.zeros(
                    (count // 2 - upward, 128), F32
                )
            if upward:
                recv_slots[n][block_at(DOWN, reach - 1, other), 0:upward, :] = jnp.zeros(
                    (upward, 128), F32
                )
    loads[0].wait()
    for load in loads[1:]:
        load.start()
    for g in range(groups):
        first = g * points
        stage_a[g, :, 0:128] = x_v[0, :, first : first + 128]
        rest = [x_v[c, :, first + 128 : first + points] for c in range(3)]
        rest.append(jnp.zeros((coefs, 128 - 3 * extra), F32))
        stage_a[g, :, 128:256] = jnp.concatenate(rest, axis=1)

    pl.semaphore_wait(barrier, groups - 1 + (2 * reach - 1) * side - 1)

    def group_copy(source, target, send, recv, to):
        return pltpu.make_async_remote_copy(
            src_ref=source,
            dst_ref=target,
            send_sem=send,
            recv_sem=recv,
            device_id=(to, part),
            device_id_type=MESH,
        )

    def group_all(room, send, recv):
        whole = room.at[pl.ds(0, groups - 1)]
        return group_copy(whole, whole, send, recv, me)

    def send_a(d, carry):
        to = group_peer(d)
        group_copy(stage_a.at[to], coef_a.at[me], a_send, a_recv, to).start()
        return carry

    def send_b(d, carry):
        to = group_peer(d)
        group_copy(stage_b.at[to], coef_b.at[me], b_send, b_recv, to).start()
        return carry

    lax.fori_loop(1, groups, send_a, 0)
    for g in range(groups):
        first = g * points
        stage_b[g, :, 0:128] = x_v[1, :, first : first + 128]
        stage_b[g, :, 128:256] = x_v[2, :, first : first + 128]
    lax.fori_loop(1, groups, send_b, 0)
    coef_a[me] = stage_a[me]
    coef_b[me] = stage_b[me]

    for load in loads[1:4]:
        load.wait()
    owner_idx = lax.broadcasted_iota(jnp.int32, (partners, 64), 0)
    slot_idx = lax.broadcasted_iota(jnp.int32, (partners, 64), 1)
    live = jnp.zeros((partners, 64), jnp.int32)
    for o in range(partners):
        live = jnp.where(owner_idx == o, pair_counts[0, o], live)
    live = slot_idx < live
    wanted = jnp.where(live, send_point[0], -1)
    fed = jnp.where(live, dest_node[0], -1).astype(F32)
    for o in range(partners):
        half = o % 2 * 64
        picks[o // 2 : o // 2 + 1, half : half + 64] = wanted[o : o + 1]
        nodes[o, :, 0:64] = fed[o : o + 1]
        nodes[o, :, 64:128] = fed[o : o + 1]

    def part_copy(source, target, send, recv, to):
        return pltpu.make_async_remote_copy(
            src_ref=source,
            dst_ref=target,
            send_sem=send,
            recv_sem=recv,
            device_id=(me, to),
            device_id_type=MESH,
        )

    def each_other(steps, act):
        def step(d, carry):
            act(lax.rem(column + d, side))
            return carry

        lax.fori_loop(0 if steps else 1, side, step, 0)

    def node_copy(way, steps, distance, other):
        landed = block_at(way, steps, column)
        to = device_at(-steps if way == DOWN else steps, other)
        owner = device_at(distance, other)
        return part_copy(
            nodes.at[owner], node_in.at[landed], node_send, node_recv, to
        )

    node_whole = node_in.at[pl.ds(0, blocks - 3)]
    node_all = part_copy(node_whole, node_whole, node_send, node_recv, part)

    for distance in DISTANCES:
        for way, steps in routes(distance):
            each_other(
                steps,
                lambda other, w=way, s=steps, d=distance: node_copy(w, s, d, other).start(),
            )
            if steps == 0:
                node_in[block_at(way, steps, column)] = nodes[device_at(distance, column)]

    for load in loads[4:8]:
        load.wait()
    lane_points = lax.broadcasted_iota(jnp.int32, (1, 256), 1)
    first_elem = me * (points // (NP * NP))

    def metric_row(r):
        row = jnp.zeros((1, 256), F32)
        for e in range(points // (NP * NP)):
            row = jnp.where(lane_points >= e * NP * NP, metrics[r, first_elem + e], row)
        return row

    for half in range(2):
        grad = grad_tables[0] * metric_row(2 * half) + grad_tables[1] * metric_row(2 * half + 1)
        high, low = split(grad)
        grad_high[:, half * 256 : half * 256 + 256] = high
        grad_low[:, half * 256 : half * 256 + 256] = low
        vel_xy[0:256, half * 256 : half * 256 + 256] = grad
    padded[128:256, :] = jnp.zeros((128, planes), F32)

    def base_step(c, carry):
        padded[0:points, :] = base_v[c, :, 0, :]
        base_t[c] = jnp.transpose(padded[...])
        base_z[c] = dot6(dz[...], base_t[c])
        flow_xy[c] = dot6(base_t[c], vel_xy[0:256, :])
        return carry

    lax.fori_loop(0, 3, base_step, 0)

    rows = pick_table.shape[0]
    point_idx = lax.broadcasted_iota(jnp.int32, (rows, 128), 0)

    def pick_step(j, carry, place, distance):
        wanted = picks[pl.ds(lax.rem(level + distance, RING) * (side // 2) + j, 1), :]
        columns = pl.ds(pl.multiple_of((place * (side // 2) + j) * 128, 128), 128)
        pick_table[:, columns] = jnp.where(point_idx == wanted, 1.0, 0.0).astype(BF16)
        return carry

    for place, distance in enumerate(DISTANCES):
        lax.fori_loop(
            0, side // 2, lambda j, c, p=place, d=distance: pick_step(j, c, p, d), 0
        )

    node_all.wait_recv()
    lane = lax.broadcasted_iota(jnp.int32, (1, 128), 1)
    left = lane < 64
    node_rows[...] = jnp.zeros((128, 128), F32)
    for j in range(blocks // 2):
        node_rows[j : j + 1, :] = jnp.where(left, node_in[2 * j], node_in[2 * j + 1])
    node_columns = jnp.transpose(node_rows[...])
    node_idx = lax.broadcasted_iota(jnp.int32, (128, NODES_OWN), 1).astype(F32)
    for j in range(blocks // 2):
        node_table[128 * j : 128 * j + 128, :] = jnp.where(
            node_idx == node_columns[:, j : j + 1], 1.0, 0.0
        ).astype(BF16)
    adv_parts[:, rows - 128 : rows] = jnp.zeros((2 * coefs, 128), BF16)

    for load in loads[8:]:
        load.wait()

    group_all(coef_a, a_send, a_recv).wait_recv()
    high, low = split(coef_a[...].reshape(planes, 256))
    both = dot3(synth_high[...], synth_low[...], high, low)
    vel[0, :, 0:128] = both[0:planes, 0:128]
    along_z[0, :, 0:128] = both[planes : 2 * planes, 0:128]
    for c in range(3):
        rest = both[:, 128:256]
        if c:
            rest = pltpu.roll(rest, 128 - c * extra, 1)
        rest = jnp.where(lane < extra, rest, 0.0)
        vel[c, :, 128:256] = rest[0:planes]
        along_z[c, :, 128:256] = rest[planes : 2 * planes]

    group_all(coef_b, b_send, b_recv).wait_recv()
    high, low = split(coef_b[...].reshape(planes, 256))
    both = dot3(synth_high[...], synth_low[...], high, low)
    for c in (1, 2):
        vel[c, :, 0:128] = both[0:planes, 128 * c - 128 : 128 * c]
        along_z[c, :, 0:128] = both[planes : 2 * planes, 128 * c - 128 : 128 * c]

    block = 32

    def advect(i):
        high, low = split(vel[i])
        vel_xy[...] = dot3(high, low, grad_high[...], grad_low[...])

        def point_step(b, carry):
            at = pl.ds(pl.multiple_of(b * block, block), block)
            total = jnp.zeros((block, 256), F32)
            for j in range(3):
                slope = along_z[i, at, :] if j == 2 else vel_xy[at, j * 256 : j * 256 + 256]
                back = base_z[j, at, :] if i == 2 else flow_xy[j, at, i * 256 : i * 256 + 256]
                total = total - base_t[j, at, :] * slope + vel[j, at, :] * back
            high, low = split(total)
            phys_high[at, :] = high
            phys_low[at, :] = low
            return carry

        lax.fori_loop(0, planes // block, point_step, 0)
        adv[...] = dot3(analysis_high[...], analysis_low[...], phys_high[...], phys_low[...])

    def back_copy(n, to):
        return group_copy(
            send_adv[n].at[to], recv_adv[n].at[me], adv_send.at[n], adv_recv.at[n], to
        )

    def send_back(n):
        _, start, count, fold, _ = CHUNKS[n]
        packed = packed_rows(count, fold)
        for m in range(groups):
            at = m * coefs + start
            send_adv[n][m, 0:count, :] = adv[at : at + count, 0:128]
            rest = adv[at : at + count, 128:256]
            merged = rest[:packed]
            for f in range(1, fold):
                piece = rest[f * packed : min((f + 1) * packed, count)]
                if piece.shape[0] < packed:
                    filler = jnp.zeros((packed - piece.shape[0], 128), F32)
                    piece = jnp.concatenate([piece, filler], axis=0)
                merged = jnp.where(lane < f * extra, merged, pltpu.roll(piece, f * extra, 1))
            send_adv[n][m, count : count + packed, :] = merged

        def step(d, carry):
            back_copy(n, group_peer(d)).start()
            return carry

        lax.fori_loop(1, groups, step, 0)
        recv_adv[n][me] = send_adv[n][me]

    stores = []

    def way_rows(n, way, steps):
        _, _, count, _, upward = CHUNKS[n]
        if steps < reach - 1 or way == HERE:
            return 0, count // 2
        return (0, upward) if way == UP else (upward, count // 2 - upward)

    def slot_copy(n, way, steps, distance, other):
        first, rows_sent = way_rows(n, way, steps)
        landed = block_at(way, steps, column)
        place = DISTANCES.index(distance) * side + other
        return part_copy(
            send_slots[n].at[place, pl.ds(first, rows_sent)],
            recv_slots[n].at[landed, pl.ds(first, rows_sent)],
            slot_send.at[n],
            slot_recv.at[int(way == HERE), n],
            device_at(-steps if way == DOWN else steps, other),
        )

    summed_here = 2 * (reach - 2) * side + side + 2 * (side - 1)

    def slots_all(n, count, here):
        whole = recv_slots[n].at[pl.ds(0, count)]
        return part_copy(whole, whole, slot_send.at[n], slot_recv.at[here, n], part)

    def each_slot_copy(n, distance, act):
        for way, steps in routes(distance):
            if way_rows(n, way, steps)[1]:
                each_other(
                    steps,
                    lambda other, w=way, s=steps: act(slot_copy(n, w, s, distance, other)),
                )

    def dense_copy(n, way):
        return part_copy(
            dense.at[way, n, pl.ds(0, CHUNKS[n][2])],
            dense_in.at[way, n, pl.ds(0, CHUNKS[n][2])],
            dense_send.at[way, n],
            dense_recv.at[way, n],
            device_at(1 if way == UP else -1, column),
        )

    wide = min(512, 128 * pairs)
    tiles = 128 * pairs // wide
    tile_owners = 2 * (wide // 128)

    def send_picked(n):
        i, start, count, fold, _ = CHUNKS[n]
        packed = packed_rows(count, fold)

        group_all(recv_adv[n], adv_send.at[n], adv_recv.at[n]).wait_recv()
        for g in range(groups):
            first = g * points
            rest = recv_adv[n][g, count : count + packed, :]
            pieces = [rest]
            for f in range(1, fold):
                piece = pltpu.roll(rest, 128 - f * extra, 1)
                pieces.append(piece[: min(packed, count - f * packed)])
            rest = jnp.concatenate(pieces, axis=0)
            advection[i, start : start + count, first : first + 128] = recv_adv[n][g, 0:count, :]
            advection[i, start : start + count, first + 128 : first + points] = rest[:, :extra]
        store = pltpu.make_async_copy(
            advection.at[i, pl.ds(start, count)],
            advection_hbm.at[i, pl.ds(start, count)],
            store_sem.at[n],
        )
        store.start()
        stores.append(store)
        high, low = split(advection[i, start : start + count, :])
        adv_parts[0:count, 0:full] = high
        adv_parts[count : 2 * count, 0:full] = low
        half = count // 2

        for t in range(tiles):
            picked = dot(adv_parts[0 : 2 * count, :], pick_table[:, t * wide : (t + 1) * wide])
            picked = picked[0:count] + picked[count : 2 * count]
            for j in range(wide // 128):
                upper = picked[0:half, j * 128 : j * 128 + 128]
                lower = picked[half:count, j * 128 : j * 128 + 128]
                place = t * tile_owners + 2 * j
                send_slots[n][place] = jnp.where(left, upper, pltpu.roll(lower, 64, 1))
                send_slots[n][place + 1] = jnp.where(left, pltpu.roll(upper, 64, 1), lower)
            for place in range(t * tile_owners // side, (t + 1) * tile_owners // side):
                distance = DISTANCES[place]
                each_slot_copy(n, distance, lambda copy: copy.start())
                for way, steps in routes(distance):
                    if steps == 0:
                        recv_slots[n][block_at(way, steps, column)] = send_slots[n][
                            place * side + column
                        ]

    def sum_blocks(n, first, last):
        count = CHUNKS[n][2]
        for j in range(first // 2, last // 2):
            even = recv_slots[n][2 * j]
            odd = recv_slots[n][2 * j + 1]
            upper = jnp.where(left, even, pltpu.roll(odd, 64, 1))
            lower = jnp.where(left, pltpu.roll(even, 64, 1), odd)
            high, low = split(jnp.concatenate([upper, lower], axis=0))
            slot_parts[0:count, j * 128 : j * 128 + 128] = high
            slot_parts[count : 2 * count, j * 128 : j * 128 + 128] = low
        summed = dot(
            slot_parts[0 : 2 * count, 64 * first : 64 * last], node_table[64 * first : 64 * last, :]
        )
        return summed[0:count] + summed[count : 2 * count]

    def pass_on(n):
        count = CHUNKS[n][2]
        slots_all(n, summed_here, 0).wait_recv()
        for way in (UP, DOWN):
            dense[way, n, 0:count, :] = sum_blocks(
                n, way * reach * side, (way + 1) * reach * side
            )
            dense_copy(n, way).start()

    def add_nodes(n):
        i, start, count, _, _ = CHUNKS[n]
        slots_all(n, side - 1, 1).wait_recv()
        here = sum_blocks(n, 2 * reach * side, blocks)
        for way in (UP, DOWN):
            dense_copy(n, way).wait_recv()
        totals[i, start : start + count, :] = (
            here + dense_in[UP, n, 0:count, :] + dense_in[DOWN, n, 0:count, :]
        )
        store = pltpu.make_async_copy(
            totals.at[i, pl.ds(start, count)],
            totals_hbm.at[i, pl.ds(start, count)],
            store_sem.at[len(CHUNKS) + n],
        )
        store.start()
        stores.append(store)

    advect(0)
    send_back(0)
    advect(1)
    send_back(1)
    advect(2)
    send_back(2)
    send_picked(0)
    send_picked(1)
    send_picked(2)
    pass_on(0)
    pass_on(1)
    add_nodes(0)
    pass_on(2)
    add_nodes(1)
    add_nodes(2)

    group_all(stage_a, a_send, a_recv).wait_send()
    group_all(stage_b, b_send, b_recv).wait_send()
    for n in range(len(CHUNKS)):
        group_all(send_adv[n], adv_send.at[n], adv_recv.at[n]).wait_send()
    node_all.wait_send()
    for n in range(len(CHUNKS)):
        slots_all(n, summed_here + side - 1, 0).wait_send()
    for n in range(len(CHUNKS)):
        for way in (UP, DOWN):
            dense_copy(n, way).wait_send()
    for store in stores:
        store.wait()


def per_device(adjoint_modes, base_planes, metrics, send_point, dest_node, pair_counts):
    components, coefs, local_points = adjoint_modes.shape
    planes = base_planes.shape[3]
    groups = lax.axis_size("modes")
    partners = lax.axis_size("elems")
    points = local_points // groups
    pairs = partners // 2
    synth, analysis, slope, dz = spectral_tables(planes)
    synth_high, synth_low = halves_of(np.concatenate([synth, slope], axis=0))
    analysis_high, analysis_low = halves_of(analysis)
    grad = gradient_tables(points // (NP * NP), 256)

    rows = -(-local_points // 128) * 128
    blocks = partners + partners // RING
    any_spec = pl.BlockSpec(memory_space=pl.ANY)

    def room(*shape, dtype=F32):
        return pltpu.VMEM(shape, dtype)

    dma = pltpu.SemaphoreType.DMA
    scratch = [
        room(3, coefs, local_points),
        room(3, points, 1, planes),
        pltpu.SMEM(metrics.shape, F32),
        room(*send_point.shape, dtype=jnp.int32),
        room(*dest_node.shape, dtype=jnp.int32),
        pltpu.SMEM(pair_counts.shape, jnp.int32),
        room(2 * planes, planes, dtype=BF16),
        room(2 * planes, planes, dtype=BF16),
        room(planes, planes),
        room(planes, planes, dtype=BF16),
        room(planes, planes, dtype=BF16),
        room(2, 256, 256),
        room(groups, coefs, 256),
        room(groups, coefs, 256),
        room(groups, coefs, 256),
        room(groups, coefs, 256),
        room(256, planes),
        room(3, planes, 256),
        room(3, planes, 256),
        room(3, planes, 512),
        room(256, 512, dtype=BF16),
        room(256, 512, dtype=BF16),
        room(pairs, 128, dtype=jnp.int32),
        room(partners, 1, 128),
        room(rows, pairs * 128, dtype=BF16),
        room(128, 128),
        room(blocks * 64, NODES_OWN, dtype=BF16),
        room(blocks, 1, 128),
        room(3, planes, 256),
        room(3, planes, 256),
        room(planes, 512),
        room(planes, 256, dtype=BF16),
        room(planes, 256, dtype=BF16),
        room(planes, 256),
        room(3, coefs, local_points),
        room(2 * coefs, rows, dtype=BF16),
        room(2 * coefs, blocks * 64, dtype=BF16),
        room(3, coefs, NODES_OWN),
        room(2, len(CHUNKS), coefs, NODES_OWN),
        room(2, len(CHUNKS), coefs, NODES_OWN),
        dma((12,)),
        dma((2 * len(CHUNKS),)),
        dma,
        dma,
        dma,
        dma,
        dma((len(CHUNKS),)),
        dma((len(CHUNKS),)),
        dma,
        dma,
        dma((len(CHUNKS),)),
        dma((2, len(CHUNKS))),
        dma((2, len(CHUNKS))),
        dma((2, len(CHUNKS))),
    ]
    for _ in range(2):
        for _, _, count, fold, _ in CHUNKS:
            scratch.append(room(groups, count + packed_rows(count, fold), 128))
    for received in (False, True):
        for _, _, count, _, _ in CHUNKS:
            scratch.append(room(blocks if received else partners, count // 2, 128))

    def kernel(*refs):
        body(groups, partners, points, *refs)

    results = pl.pallas_call(
        kernel,
        out_shape=(
            jax.ShapeDtypeStruct((3, coefs, local_points), F32),
            jax.ShapeDtypeStruct((3, coefs, NODES_OWN), F32),
        ),
        in_specs=[any_spec] * 12,
        out_specs=(any_spec, any_spec),
        scratch_shapes=scratch,
        compiler_params=pltpu.CompilerParams(
            collective_id=0, has_side_effects=True, vmem_limit_bytes=56 * 1024 * 1024
        ),
    )(
        adjoint_modes,
        jnp.transpose(base_planes, (0, 2, 1, 3)),
        metrics,
        send_point,
        dest_node,
        pair_counts,
        synth_high,
        synth_low,
        jnp.asarray(dz, dtype=F32),
        analysis_high,
        analysis_low,
        grad,
    )

    def hand_over(advection, totals, advection_out, totals_out, held, held_totals, sem_in, sem_out):
        pieces = [
            (advection.at[c], held.at[c], advection_out.at[c]) for c in range(components)
        ] + [(totals, held_totals, totals_out)]
        loads = [
            pltpu.make_async_copy(source, middle, sem_in.at[i])
            for i, (source, middle, _) in enumerate(pieces)
        ]
        stores = [
            pltpu.make_async_copy(middle, target, sem_out.at[i])
            for i, (_, middle, target) in enumerate(pieces)
        ]
        for load in loads:
            load.start()
        for load, store in zip(loads, stores):
            load.wait()
            store.start()
        for store in stores:
            store.wait()

    return pl.pallas_call(
        hand_over,
        out_shape=tuple(jax.ShapeDtypeStruct(r.shape, r.dtype) for r in results),
        in_specs=[any_spec, any_spec],
        out_specs=(any_spec, any_spec),
        scratch_shapes=[room(*r.shape) for r in results] + [dma((components + 1,))] * 2,
        compiler_params=pltpu.CompilerParams(vmem_limit_bytes=56 * 1024 * 1024),
    )(*results)


def solution(mesh):
    return jax.shard_map(
        per_device,
        mesh=mesh,
        in_specs=(
            P(None, "modes", "elems"),
            P(None, "modes", "elems", None),
            P(None, "elems"),
            P("elems", None, None),
            P("elems", None, None),
            P("elems", None),
        ),
        out_specs=(P(None, "modes", "elems"), P(None, "modes", "elems")),
        check_vma=False,
    )
```

```python
import jax
import jax.numpy as jnp
import numpy as np
from jax import lax
from jax.experimental import pallas as pl
from jax.experimental.pallas import tpu as pltpu
from jax.sharding import PartitionSpec as P

NP = 9
NODES_OWN = 512
MESH = pl.DeviceIdType.MESH
F32 = jnp.float32
BF16 = jnp.bfloat16

span_wavenumber = 0.4

CHUNKS = ((0, 0, 32, 2, 8), (0, 32, 32, 2, 8), (1, 0, 64, 3, 16), (2, 0, 64, 3, 16))

RING = 8
UP, DOWN, HERE = 0, 1, 2
DISTANCES = (4, 3, 5, 2, 6, 1, 7, 0)


def routes(distance):
    if distance == 0:
        return ((HERE, 0),)
    if 2 * distance == RING:
        return ((UP, distance - 1), (DOWN, distance - 1))
    if 2 * distance < RING:
        return ((UP, distance - 1),)
    return ((DOWN, RING - distance - 1),)


CUTS = 1


def packed_rows(count, fold):
    return -(-count // (8 * fold)) * 8


def chebyshev_table(count):
    degree = count - 1
    position = np.arange(count)
    node_x = np.cos(np.pi * position / degree)
    weights = np.where((position == 0) | (position == degree), 2.0, 1.0)
    sign_terms = (-1.0) ** position
    identity = np.eye(count)
    spacing = node_x[:, None] - node_x[None, :] + identity
    matrix = (
        weights[:, None] * sign_terms[:, None] / (weights[None, :] * sign_terms[None, :]) / spacing
    )
    matrix = matrix * (1.0 - identity)
    matrix = matrix - identity * matrix.sum(axis=1)[:, None]
    return matrix


def spectral_tables(planes):
    position = np.arange(planes)
    wavenumber = np.where(position == 1, planes // 2, position // 2)
    angles = 2.0 * np.pi / planes * (position[:, None] * wavenumber[None, :] % planes)
    sine_col = (position % 2 == 1) & (position != 1)
    synth_table = np.where(sine_col[None, :], np.sin(angles), np.cos(angles))
    weighting = np.where(position <= 1, 1.0, 2.0) / planes
    analysis = synth_table.T * weighting[:, None]
    speeds = span_wavenumber * wavenumber
    slope_table = np.where(
        position[None, :] <= 1,
        0.0,
        np.where(
            sine_col[None, :], speeds[None, :] * np.cos(angles), -speeds[None, :] * np.sin(angles)
        ),
    )
    return synth_table, analysis, slope_table, slope_table @ analysis


def halves_of(table):
    single = table.astype(np.float32)
    high = single.astype(BF16)
    low = (single - high.astype(np.float32)).astype(BF16)
    return high, low


def gradient_tables(sub_elems, width):
    diff = chebyshev_table(NP)
    points = sub_elems * NP * NP
    tables = np.zeros((2, width, width), np.float32)
    along = (np.kron(diff, np.eye(NP)), np.kron(np.eye(NP), diff))
    for direction in range(2):
        for elem in range(sub_elems):
            rows = slice(elem * NP * NP, (elem + 1) * NP * NP)
            tables[direction, rows, rows] = along[direction].T
    assert points <= width
    return tables


def split(value):
    high = value.astype(BF16)
    return high, (value - high.astype(F32)).astype(BF16)


def dot(left, right):
    return jnp.dot(left, right, preferred_element_type=F32)


def dot3(left_high, left_low, right_high, right_low):
    return dot(left_high, right_high) + (dot(left_high, right_low) + dot(left_low, right_high))


def dot6(left, right):
    return jnp.dot(left, right, precision=lax.Precision.HIGHEST, preferred_element_type=F32)


def body(
    groups,
    partners,
    points,
    x_hbm,
    base_hbm,
    metrics_hbm,
    send_point_hbm,
    dest_node_hbm,
    pair_counts_hbm,
    synth_high_hbm,
    synth_low_hbm,
    dz_hbm,
    analysis_high_hbm,
    analysis_low_hbm,
    grad_hbm,
    advection_hbm,
    totals_hbm,
    x_v,
    base_v,
    metrics,
    send_point,
    dest_node,
    pair_counts,
    synth_high,
    synth_low,
    dz,
    analysis_high,
    analysis_low,
    grad_tables,
    stage_a,
    stage_b,
    coef_a,
    coef_b,
    padded,
    base_t,
    base_z,
    flow_xy,
    grad_high,
    grad_low,
    picks,
    nodes,
    pick_table,
    node_rows,
    node_table,
    node_in,
    vel,
    along_z,
    vel_xy,
    phys_high,
    phys_low,
    adv,
    advection,
    adv_parts,
    slot_parts,
    totals,
    dense,
    dense_in,
    load_sem,
    store_sem,
    a_send,
    a_recv,
    b_send,
    b_recv,
    adv_send,
    adv_recv,
    node_send,
    node_recv,
    slot_send,
    slot_recv,
    dense_send,
    dense_recv,
    *chunk_rooms,
):
    send_adv, recv_adv, send_slots, recv_slots = (
        chunk_rooms[i * len(CHUNKS) : (i + 1) * len(CHUNKS)] for i in range(4)
    )
    me = lax.axis_index("modes")
    part = lax.axis_index("elems")
    planes = dz.shape[0]
    coefs = planes // groups
    extra = points - 128
    pairs = partners // 2
    full = groups * points
    side = partners // RING
    level = part // side
    column = lax.rem(part, side)
    reach = RING // 2
    blocks = 2 * reach * side + side

    def device_at(steps, other):
        return lax.rem(level + steps + RING, RING) * side + other

    def block_at(way, steps, other):
        return (way * reach + steps) * side + other

    barrier = pltpu.get_barrier_semaphore()

    def group_peer(d):
        return lax.rem(me + d, groups)

    def greet_group(d, carry):
        pl.semaphore_signal(barrier, inc=1, device_id=(group_peer(d), part), device_id_type=MESH)
        return carry

    def greet_part(d, carry):
        to = device_at(d // side - reach + 1, lax.rem(d, side))

        @pl.when(to != part)
        def _():
            pl.semaphore_signal(barrier, inc=1, device_id=(me, to), device_id_type=MESH)

        return carry

    lax.fori_loop(1, groups, greet_group, 0)
    lax.fori_loop(0, (2 * reach - 1) * side, greet_part, 0)

    loads = [
        pltpu.make_async_copy(source, target, load_sem.at[i])
        for i, (source, target) in enumerate(
            (
                *(
                    (x_hbm.at[c, pl.ds(r, 16)], x_v.at[c, pl.ds(r, 16)])
                    for c in range(3)
                    for r in range(0, coefs, 16)
                ),
                (send_point_hbm, send_point),
                (dest_node_hbm, dest_node),
                (pair_counts_hbm, pair_counts),
                (metrics_hbm, metrics),
                (base_hbm, base_v),
                (grad_hbm, grad_tables),
                (dz_hbm, dz),
                (synth_high_hbm, synth_high),
                (synth_low_hbm, synth_low),
                (analysis_high_hbm, analysis_high),
                (analysis_low_hbm, analysis_low),
            )
        )
    ]
    cuts = 3 * coefs // 16
    for load in loads[:cuts]:
        load.start()

    for n, (_, _, count, _, upward) in enumerate(CHUNKS):
        for other in range(side):
            if upward < count // 2:
                recv_slots[n][block_at(UP, reach - 1, other), upward : count // 2, :] = jnp.zeros(
                    (count // 2 - upward, 128), F32
                )
            if upward:
                recv_slots[n][block_at(DOWN, reach - 1, other), 0:upward, :] = jnp.zeros(
                    (upward, 128), F32
                )
    for load in loads[:cuts]:
        load.wait()
    for load in loads[cuts:]:
        load.start()
    loads = loads[cuts:]
    for g in range(groups):
        first = g * points
        stage_a[g, :, 0:128] = x_v[0, :, first : first + 128]
        rest = [x_v[c, :, first + 128 : first + points] for c in range(3)]
        rest.append(jnp.zeros((coefs, 128 - 3 * extra), F32))
        stage_a[g, :, 128:256] = jnp.concatenate(rest, axis=1)

    pl.semaphore_wait(barrier, groups - 1 + (2 * reach - 1) * side - 1)

    def group_copy(source, target, send, recv, to):
        return pltpu.make_async_remote_copy(
            src_ref=source,
            dst_ref=target,
            send_sem=send,
            recv_sem=recv,
            device_id=(to, part),
            device_id_type=MESH,
        )

    def group_all(room, send, recv):
        whole = room.at[pl.ds(0, groups - 1)]
        return group_copy(whole, whole, send, recv, me)

    def send_a(d, carry):
        to = group_peer(d)
        group_copy(stage_a.at[to], coef_a.at[me], a_send, a_recv, to).start()
        return carry

    def send_b(d, carry):
        to = group_peer(d)
        group_copy(stage_b.at[to], coef_b.at[me], b_send, b_recv, to).start()
        return carry

    lax.fori_loop(1, groups, send_a, 0)
    for g in range(groups):
        first = g * points
        stage_b[g, :, 0:128] = x_v[1, :, first : first + 128]
        stage_b[g, :, 128:256] = x_v[2, :, first : first + 128]
    lax.fori_loop(1, groups, send_b, 0)
    coef_a[me] = stage_a[me]
    coef_b[me] = stage_b[me]

    for load in loads[0:3]:
        load.wait()
    owner_idx = lax.broadcasted_iota(jnp.int32, (partners, 64), 0)
    slot_idx = lax.broadcasted_iota(jnp.int32, (partners, 64), 1)
    live = jnp.zeros((partners, 64), jnp.int32)
    for o in range(partners):
        live = jnp.where(owner_idx == o, pair_counts[0, o], live)
    live = slot_idx < live
    wanted = jnp.where(live, send_point[0], -1)
    fed = jnp.where(live, dest_node[0], -1).astype(F32)
    for o in range(partners):
        half = o % 2 * 64
        picks[o // 2 : o // 2 + 1, half : half + 64] = wanted[o : o + 1]
        nodes[o, :, 0:64] = fed[o : o + 1]
        nodes[o, :, 64:128] = fed[o : o + 1]

    def part_copy(source, target, send, recv, to):
        return pltpu.make_async_remote_copy(
            src_ref=source,
            dst_ref=target,
            send_sem=send,
            recv_sem=recv,
            device_id=(me, to),
            device_id_type=MESH,
        )

    def each_other(steps, act):
        def step(d, carry):
            act(lax.rem(column + d, side))
            return carry

        lax.fori_loop(0 if steps else 1, side, step, 0)

    def node_copy(way, steps, distance, other):
        landed = block_at(way, steps, column)
        to = device_at(-steps if way == DOWN else steps, other)
        owner = device_at(distance, other)
        return part_copy(
            nodes.at[owner], node_in.at[landed], node_send, node_recv, to
        )

    node_whole = node_in.at[pl.ds(0, blocks - 3)]
    node_all = part_copy(node_whole, node_whole, node_send, node_recv, part)

    for distance in DISTANCES:
        for way, steps in routes(distance):
            each_other(
                steps,
                lambda other, w=way, s=steps, d=distance: node_copy(w, s, d, other).start(),
            )
            if steps == 0:
                node_in[block_at(way, steps, column)] = nodes[device_at(distance, column)]

    for load in loads[3:7]:
        load.wait()
    lane_points = lax.broadcasted_iota(jnp.int32, (1, 256), 1)
    first_elem = me * (points // (NP * NP))

    def metric_row(r):
        row = jnp.zeros((1, 256), F32)
        for e in range(points // (NP * NP)):
            row = jnp.where(lane_points >= e * NP * NP, metrics[r, first_elem + e], row)
        return row

    for half in range(2):
        grad = grad_tables[0] * metric_row(2 * half) + grad_tables[1] * metric_row(2 * half + 1)
        high, low = split(grad)
        grad_high[:, half * 256 : half * 256 + 256] = high
        grad_low[:, half * 256 : half * 256 + 256] = low
        vel_xy[0:256, half * 256 : half * 256 + 256] = grad
    padded[128:256, :] = jnp.zeros((128, planes), F32)

    def base_step(c, carry):
        padded[0:points, :] = base_v[c, :, 0, :]
        base_t[c] = jnp.transpose(padded[...])
        base_z[c] = dot6(dz[...], base_t[c])
        flow_xy[c] = dot6(base_t[c], vel_xy[0:256, :])
        return carry

    lax.fori_loop(0, 3, base_step, 0)

    rows = pick_table.shape[0]
    point_idx = lax.broadcasted_iota(jnp.int32, (rows, 128), 0)

    def pick_step(j, carry, place, distance):
        wanted = picks[pl.ds(lax.rem(level + distance, RING) * (side // 2) + j, 1), :]
        columns = pl.ds(pl.multiple_of((place * (side // 2) + j) * 128, 128), 128)
        pick_table[:, columns] = jnp.where(point_idx == wanted, 1.0, 0.0).astype(BF16)
        return carry

    for place, distance in enumerate(DISTANCES):
        lax.fori_loop(
            0, side // 2, lambda j, c, p=place, d=distance: pick_step(j, c, p, d), 0
        )

    node_all.wait_recv()
    lane = lax.broadcasted_iota(jnp.int32, (1, 128), 1)
    left = lane < 64
    node_rows[...] = jnp.zeros((128, 128), F32)
    for j in range(blocks // 2):
        node_rows[j : j + 1, :] = jnp.where(left, node_in[2 * j], node_in[2 * j + 1])
    node_columns = jnp.transpose(node_rows[...])
    node_idx = lax.broadcasted_iota(jnp.int32, (128, NODES_OWN), 1).astype(F32)
    for j in range(blocks // 2):
        node_table[128 * j : 128 * j + 128, :] = jnp.where(
            node_idx == node_columns[:, j : j + 1], 1.0, 0.0
        ).astype(BF16)
    adv_parts[:, rows - 128 : rows] = jnp.zeros((2 * coefs, 128), BF16)

    for load in loads[7:]:
        load.wait()

    group_all(coef_a, a_send, a_recv).wait_recv()
    high, low = split(coef_a[...].reshape(planes, 256))
    both = dot3(synth_high[...], synth_low[...], high, low)
    vel[0, :, 0:128] = both[0:planes, 0:128]
    along_z[0, :, 0:128] = both[planes : 2 * planes, 0:128]
    for c in range(3):
        rest = both[:, 128:256]
        if c:
            rest = pltpu.roll(rest, 128 - c * extra, 1)
        rest = jnp.where(lane < extra, rest, 0.0)
        vel[c, :, 128:256] = rest[0:planes]
        along_z[c, :, 128:256] = rest[planes : 2 * planes]

    block = 32

    def first_pass(i):
        high, low = split(vel[i])
        vel_xy[...] = dot3(high, low, grad_high[...], grad_low[...])

        def point_step(b, carry):
            at = pl.ds(pl.multiple_of(b * block, block), block)
            total = vel[i, at, :] * flow_back(i, i, at)
            for j in range(3):
                slope = along_z[i, at, :] if j == 2 else vel_xy[at, j * 256 : j * 256 + 256]
                total = total - base_t[j, at, :] * slope
            adv[at, :] = total
            return carry

        lax.fori_loop(0, planes // block, point_step, 0)

    def flow_back(i, j, at):
        return base_z[j, at, :] if i == 2 else flow_xy[j, at, i * 256 : i * 256 + 256]

    first_pass(0)
    group_all(coef_b, b_send, b_recv).wait_recv()

    def second_half(rows, target):
        high, low = split(coef_b[...].reshape(planes, 256))
        part_b = dot3(synth_high[rows, :], synth_low[rows, :], high, low)
        target[1, :, 0:128] = part_b[:, 0:128]
        target[2, :, 0:128] = part_b[:, 128:256]

    second_half(slice(0, planes), vel)

    def advect(i):
        if i:
            first_pass(i)

        def point_step(b, carry):
            at = pl.ds(pl.multiple_of(b * block, block), block)
            total = adv[at, :]
            for j in range(3):
                if j != i:
                    total = total + vel[j, at, :] * flow_back(i, j, at)
            high, low = split(total)
            phys_high[at, :] = high
            phys_low[at, :] = low
            return carry

        lax.fori_loop(0, planes // block, point_step, 0)
        adv[...] = dot3(analysis_high[...], analysis_low[...], phys_high[...], phys_low[...])

    def back_copy(n, to):
        return group_copy(
            send_adv[n].at[to], recv_adv[n].at[me], adv_send.at[n], adv_recv.at[n], to
        )

    def send_back(n):
        _, start, count, fold, _ = CHUNKS[n]
        packed = packed_rows(count, fold)
        for m in range(groups):
            at = m * coefs + start
            send_adv[n][m, 0:count, :] = adv[at : at + count, 0:128]
            rest = adv[at : at + count, 128:256]
            merged = rest[:packed]
            for f in range(1, fold):
                piece = rest[f * packed : min((f + 1) * packed, count)]
                if piece.shape[0] < packed:
                    filler = jnp.zeros((packed - piece.shape[0], 128), F32)
                    piece = jnp.concatenate([piece, filler], axis=0)
                merged = jnp.where(lane < f * extra, merged, pltpu.roll(piece, f * extra, 1))
            send_adv[n][m, count : count + packed, :] = merged

        def step(d, carry):
            back_copy(n, group_peer(d)).start()
            return carry

        lax.fori_loop(1, groups, step, 0)
        recv_adv[n][me] = send_adv[n][me]

    stores = []

    def late_slopes():
        second_half(slice(planes, 2 * planes), along_z)

    def way_rows(n, way, steps):
        _, _, count, _, upward = CHUNKS[n]
        if steps < reach - 1 or way == HERE:
            return 0, count // 2
        return (0, upward) if way == UP else (upward, count // 2 - upward)

    def slot_copy(n, way, steps, distance, other):
        first, rows_sent = way_rows(n, way, steps)
        landed = block_at(way, steps, column)
        place = DISTANCES.index(distance) * side + other
        return part_copy(
            send_slots[n].at[place, pl.ds(first, rows_sent)],
            recv_slots[n].at[landed, pl.ds(first, rows_sent)],
            slot_send.at[n],
            slot_recv.at[int(way == HERE), n],
            device_at(-steps if way == DOWN else steps, other),
        )

    summed_here = 2 * (reach - 2) * side + side + 2 * (side - 1)

    def slots_all(n, count, here):
        whole = recv_slots[n].at[pl.ds(0, count)]
        return part_copy(whole, whole, slot_send.at[n], slot_recv.at[here, n], part)

    def each_slot_copy(n, distance, act):
        for way, steps in routes(distance):
            if way_rows(n, way, steps)[1]:
                each_other(
                    steps,
                    lambda other, w=way, s=steps: act(slot_copy(n, w, s, distance, other)),
                )

    def dense_copy(n, way):
        return part_copy(
            dense.at[way, n, pl.ds(0, CHUNKS[n][2])],
            dense_in.at[way, n, pl.ds(0, CHUNKS[n][2])],
            dense_send.at[way, n],
            dense_recv.at[way, n],
            device_at(1 if way == UP else -1, column),
        )

    wide = min(512, 128 * pairs)
    tiles = 128 * pairs // wide
    tile_owners = 2 * (wide // 128)

    def send_picked(n):
        i, start, count, fold, _ = CHUNKS[n]
        packed = packed_rows(count, fold)

        group_all(recv_adv[n], adv_send.at[n], adv_recv.at[n]).wait_recv()
        for g in range(groups):
            first = g * points
            rest = recv_adv[n][g, count : count + packed, :]
            pieces = [rest]
            for f in range(1, fold):
                piece = pltpu.roll(rest, 128 - f * extra, 1)
                pieces.append(piece[: min(packed, count - f * packed)])
            rest = jnp.concatenate(pieces, axis=0)
            advection[i, start : start + count, first : first + 128] = recv_adv[n][g, 0:count, :]
            advection[i, start : start + count, first + 128 : first + points] = rest[:, :extra]
        store = pltpu.make_async_copy(
            advection.at[i, pl.ds(start, count)],
            advection_hbm.at[i, pl.ds(start, count)],
            store_sem.at[n],
        )
        store.start()
        stores.append(store)
        high, low = split(advection[i, start : start + count, :])
        adv_parts[0:count, 0:full] = high
        adv_parts[count : 2 * count, 0:full] = low
        half = count // 2

        for t in range(tiles):
            picked = dot(adv_parts[0 : 2 * count, :], pick_table[:, t * wide : (t + 1) * wide])
            picked = picked[0:count] + picked[count : 2 * count]
            for j in range(wide // 128):
                upper = picked[0:half, j * 128 : j * 128 + 128]
                lower = picked[half:count, j * 128 : j * 128 + 128]
                place = t * tile_owners + 2 * j
                send_slots[n][place] = jnp.where(left, upper, pltpu.roll(lower, 64, 1))
                send_slots[n][place + 1] = jnp.where(left, pltpu.roll(upper, 64, 1), lower)
            for place in range(t * tile_owners // side, (t + 1) * tile_owners // side):
                distance = DISTANCES[place]
                each_slot_copy(n, distance, lambda copy: copy.start())
                for way, steps in routes(distance):
                    if steps == 0:
                        recv_slots[n][block_at(way, steps, column)] = send_slots[n][
                            place * side + column
                        ]

    def sum_blocks(n, first, last):
        count = CHUNKS[n][2]
        for j in range(first // 2, last // 2):
            even = recv_slots[n][2 * j]
            odd = recv_slots[n][2 * j + 1]
            upper = jnp.where(left, even, pltpu.roll(odd, 64, 1))
            lower = jnp.where(left, pltpu.roll(even, 64, 1), odd)
            high, low = split(jnp.concatenate([upper, lower], axis=0))
            slot_parts[0:count, j * 128 : j * 128 + 128] = high
            slot_parts[count : 2 * count, j * 128 : j * 128 + 128] = low
        summed = dot(
            slot_parts[0 : 2 * count, 64 * first : 64 * last], node_table[64 * first : 64 * last, :]
        )
        return summed[0:count] + summed[count : 2 * count]

    def pass_on(n):
        count = CHUNKS[n][2]
        slots_all(n, summed_here, 0).wait_recv()
        for way in (UP, DOWN):
            dense[way, n, 0:count, :] = sum_blocks(
                n, way * reach * side, (way + 1) * reach * side
            )
            dense_copy(n, way).start()

    def add_nodes(n):
        i, start, count, _, _ = CHUNKS[n]
        slots_all(n, side - 1, 1).wait_recv()
        here = sum_blocks(n, 2 * reach * side, blocks)
        for way in (UP, DOWN):
            dense_copy(n, way).wait_recv()
        totals[i, start : start + count, :] = (
            here + dense_in[UP, n, 0:count, :] + dense_in[DOWN, n, 0:count, :]
        )
        store = pltpu.make_async_copy(
            totals.at[i, pl.ds(start, count)],
            totals_hbm.at[i, pl.ds(start, count)],
            store_sem.at[len(CHUNKS) + n],
        )
        store.start()
        stores.append(store)

    advect(0)
    send_back(0)
    send_back(1)
    late_slopes()
    advect(1)
    send_back(2)
    send_picked(0)
    advect(2)
    send_back(3)
    send_picked(1)
    send_picked(2)
    send_picked(3)
    pass_on(0)
    pass_on(1)
    pass_on(2)
    pass_on(3)
    add_nodes(0)
    add_nodes(1)
    add_nodes(2)
    add_nodes(3)

    group_all(stage_a, a_send, a_recv).wait_send()
    group_all(stage_b, b_send, b_recv).wait_send()
    for n in range(len(CHUNKS)):
        group_all(send_adv[n], adv_send.at[n], adv_recv.at[n]).wait_send()
    node_all.wait_send()
    for n in range(len(CHUNKS)):
        slots_all(n, summed_here + side - 1, 0).wait_send()
    for n in range(len(CHUNKS)):
        for way in (UP, DOWN):
            dense_copy(n, way).wait_send()
    for store in stores:
        store.wait()


def per_device(adjoint_modes, base_planes, metrics, send_point, dest_node, pair_counts):
    components, coefs, local_points = adjoint_modes.shape
    planes = base_planes.shape[3]
    groups = lax.axis_size("modes")
    partners = lax.axis_size("elems")
    points = local_points // groups
    pairs = partners // 2
    synth, analysis, slope, dz = spectral_tables(planes)
    synth_high, synth_low = halves_of(np.concatenate([synth, slope], axis=0))
    analysis_high, analysis_low = halves_of(analysis)
    grad = gradient_tables(points // (NP * NP), 256)

    rows = -(-local_points // 128) * 128
    blocks = partners + partners // RING
    any_spec = pl.BlockSpec(memory_space=pl.ANY)

    def room(*shape, dtype=F32):
        return pltpu.VMEM(shape, dtype)

    dma = pltpu.SemaphoreType.DMA
    scratch = [
        room(3, coefs, local_points),
        room(3, points, 1, planes),
        pltpu.SMEM(metrics.shape, F32),
        room(*send_point.shape, dtype=jnp.int32),
        room(*dest_node.shape, dtype=jnp.int32),
        pltpu.SMEM(pair_counts.shape, jnp.int32),
        room(2 * planes, planes, dtype=BF16),
        room(2 * planes, planes, dtype=BF16),
        room(planes, planes),
        room(planes, planes, dtype=BF16),
        room(planes, planes, dtype=BF16),
        room(2, 256, 256),
        room(groups, coefs, 256),
        room(groups, coefs, 256),
        room(groups, coefs, 256),
        room(groups, coefs, 256),
        room(256, planes),
        room(3, planes, 256),
        room(3, planes, 256),
        room(3, planes, 512),
        room(256, 512, dtype=BF16),
        room(256, 512, dtype=BF16),
        room(pairs, 128, dtype=jnp.int32),
        room(partners, 1, 128),
        room(rows, pairs * 128, dtype=BF16),
        room(128, 128),
        room(blocks * 64, NODES_OWN, dtype=BF16),
        room(blocks, 1, 128),
        room(3, planes, 256),
        room(3, planes, 256),
        room(planes, 512),
        room(planes, 256, dtype=BF16),
        room(planes, 256, dtype=BF16),
        room(planes, 256),
        room(3, coefs, local_points),
        room(2 * coefs, rows, dtype=BF16),
        room(2 * coefs, blocks * 64, dtype=BF16),
        room(3, coefs, NODES_OWN),
        room(2, len(CHUNKS), coefs, NODES_OWN),
        room(2, len(CHUNKS), coefs, NODES_OWN),
        dma((11 + 3 * coefs // 16,)),
        dma((2 * len(CHUNKS),)),
        dma,
        dma,
        dma,
        dma,
        dma((len(CHUNKS),)),
        dma((len(CHUNKS),)),
        dma,
        dma,
        dma((len(CHUNKS),)),
        dma((2, len(CHUNKS))),
        dma((2, len(CHUNKS))),
        dma((2, len(CHUNKS))),
    ]
    for _ in range(2):
        for _, _, count, fold, _ in CHUNKS:
            scratch.append(room(groups, count + packed_rows(count, fold), 128))
    for received in (False, True):
        for _, _, count, _, _ in CHUNKS:
            scratch.append(room(blocks if received else partners, count // 2, 128))

    def kernel(*refs):
        body(groups, partners, points, *refs)

    results = pl.pallas_call(
        kernel,
        out_shape=(
            jax.ShapeDtypeStruct((3, coefs, local_points), F32),
            jax.ShapeDtypeStruct((3, coefs, NODES_OWN), F32),
        ),
        in_specs=[any_spec] * 12,
        out_specs=(any_spec, any_spec),
        scratch_shapes=scratch,
        compiler_params=pltpu.CompilerParams(
            collective_id=0, has_side_effects=True, vmem_limit_bytes=56 * 1024 * 1024
        ),
    )(
        adjoint_modes,
        jnp.transpose(base_planes, (0, 2, 1, 3)),
        metrics,
        send_point,
        dest_node,
        pair_counts,
        synth_high,
        synth_low,
        jnp.asarray(dz, dtype=F32),
        analysis_high,
        analysis_low,
        grad,
    )

    def hand_over(advection, totals, advection_out, totals_out, held, held_totals, sem_in, sem_out):
        pieces = [
            tuple(room.at[c, pl.ds(r, coefs // CUTS)] for room in rooms)
            for rooms in ((advection, held, advection_out), (totals, held_totals, totals_out))
            for c in range(components)
            for r in range(0, coefs, coefs // CUTS)
        ]
        loads = [
            pltpu.make_async_copy(source, middle, sem_in.at[i])
            for i, (source, middle, _) in enumerate(pieces)
        ]
        stores = [
            pltpu.make_async_copy(middle, target, sem_out.at[i])
            for i, (_, middle, target) in enumerate(pieces)
        ]
        for load in loads:
            load.start()
        for load, store in zip(loads, stores):
            load.wait()
            store.start()
        for store in stores:
            store.wait()

    return pl.pallas_call(
        hand_over,
        out_shape=tuple(jax.ShapeDtypeStruct(r.shape, r.dtype) for r in results),
        in_specs=[any_spec, any_spec],
        out_specs=(any_spec, any_spec),
        scratch_shapes=[room(*r.shape) for r in results] + [dma((2 * components * CUTS,))] * 2,
        compiler_params=pltpu.CompilerParams(vmem_limit_bytes=56 * 1024 * 1024),
    )(*results)


def solution(mesh):
    return jax.shard_map(
        per_device,
        mesh=mesh,
        in_specs=(
            P(None, "modes", "elems"),
            P(None, "modes", "elems", None),
            P(None, "elems"),
            P("elems", None, None),
            P("elems", None, None),
            P("elems", None),
        ),
        out_specs=(P(None, "modes", "elems"), P(None, "modes", "elems")),
        check_vma=False,
    )
```

```python
import jax
import jax.numpy as jnp
import numpy as np
from jax import lax
from jax.experimental import pallas as pl
from jax.experimental.pallas import tpu as pltpu
from jax.sharding import PartitionSpec as P

NP = 9
NODES_OWN = 512
MESH = pl.DeviceIdType.MESH
F32 = jnp.float32
BF16 = jnp.bfloat16

span_wavenumber = 0.4

CHUNKS = ((0, 0, 32, 2, 8), (0, 32, 32, 2, 8), (1, 0, 64, 3, 16), (2, 0, 64, 3, 16))

RING = 8
UP, DOWN, HERE = 0, 1, 2
DISTANCES = (4, 3, 5, 2, 6, 1, 7, 0)


def routes(distance):
    if distance == 0:
        return ((HERE, 0),)
    if 2 * distance == RING:
        return ((UP, distance - 1), (DOWN, distance - 1))
    if 2 * distance < RING:
        return ((UP, distance - 1),)
    return ((DOWN, RING - distance - 1),)


CUTS = 1


def packed_rows(count, fold):
    return -(-count // (8 * fold)) * 8


def chebyshev_table(count):
    degree = count - 1
    position = np.arange(count)
    node_x = np.cos(np.pi * position / degree)
    weights = np.where((position == 0) | (position == degree), 2.0, 1.0)
    sign_terms = (-1.0) ** position
    identity = np.eye(count)
    spacing = node_x[:, None] - node_x[None, :] + identity
    matrix = (
        weights[:, None] * sign_terms[:, None] / (weights[None, :] * sign_terms[None, :]) / spacing
    )
    matrix = matrix * (1.0 - identity)
    matrix = matrix - identity * matrix.sum(axis=1)[:, None]
    return matrix


def spectral_tables(planes):
    position = np.arange(planes)
    wavenumber = np.where(position == 1, planes // 2, position // 2)
    angles = 2.0 * np.pi / planes * (position[:, None] * wavenumber[None, :] % planes)
    sine_col = (position % 2 == 1) & (position != 1)
    synth_table = np.where(sine_col[None, :], np.sin(angles), np.cos(angles))
    weighting = np.where(position <= 1, 1.0, 2.0) / planes
    analysis = synth_table.T * weighting[:, None]
    speeds = span_wavenumber * wavenumber
    slope_table = np.where(
        position[None, :] <= 1,
        0.0,
        np.where(
            sine_col[None, :], speeds[None, :] * np.cos(angles), -speeds[None, :] * np.sin(angles)
        ),
    )
    return synth_table, analysis, slope_table, slope_table @ analysis


def halves_of(table):
    single = table.astype(np.float32)
    high = single.astype(BF16)
    low = (single - high.astype(np.float32)).astype(BF16)
    return high, low


def gradient_tables(sub_elems, width):
    diff = chebyshev_table(NP)
    points = sub_elems * NP * NP
    tables = np.zeros((2, width, width), np.float32)
    along = (np.kron(diff, np.eye(NP)), np.kron(np.eye(NP), diff))
    for direction in range(2):
        for elem in range(sub_elems):
            rows = slice(elem * NP * NP, (elem + 1) * NP * NP)
            tables[direction, rows, rows] = along[direction].T
    assert points <= width
    return tables


def split(value):
    high = value.astype(BF16)
    return high, (value - high.astype(F32)).astype(BF16)


def dot(left, right):
    return jnp.dot(left, right, preferred_element_type=F32)


def dot3(left_high, left_low, right_high, right_low):
    return dot(left_high, right_high) + (dot(left_high, right_low) + dot(left_low, right_high))


def dot6(left, right):
    return jnp.dot(left, right, precision=lax.Precision.HIGHEST, preferred_element_type=F32)


def body(
    groups,
    partners,
    points,
    x_hbm,
    base_hbm,
    metrics_hbm,
    send_point_hbm,
    dest_node_hbm,
    pair_counts_hbm,
    synth_high_hbm,
    synth_low_hbm,
    dz_hbm,
    analysis_high_hbm,
    analysis_low_hbm,
    grad_hbm,
    advection_hbm,
    totals_hbm,
    x_v,
    base_v,
    metrics,
    send_point,
    dest_node,
    pair_counts,
    synth_high,
    synth_low,
    dz,
    analysis_high,
    analysis_low,
    grad_tables,
    stage_a,
    stage_b,
    coef_a,
    coef_b,
    padded,
    base_t,
    base_z,
    flow_xy,
    grad_high,
    grad_low,
    picks,
    nodes,
    pick_table,
    node_rows,
    node_table,
    node_in,
    vel,
    along_z,
    vel_xy,
    phys_high,
    phys_low,
    adv,
    advection,
    adv_parts,
    slot_parts,
    totals,
    dense,
    dense_in,
    load_sem,
    store_sem,
    a_send,
    a_recv,
    b_send,
    b_recv,
    adv_send,
    adv_recv,
    node_send,
    node_recv,
    slot_send,
    slot_recv,
    dense_send,
    dense_recv,
    ready_sem,
    go_sem,
    *chunk_rooms,
):
    send_adv, recv_adv, send_slots, recv_slots = (
        chunk_rooms[i * len(CHUNKS) : (i + 1) * len(CHUNKS)] for i in range(4)
    )
    me = lax.axis_index("modes")
    part = lax.axis_index("elems")
    planes = dz.shape[0]
    coefs = planes // groups
    extra = points - 128
    pairs = partners // 2
    full = groups * points
    side = partners // RING
    level = part // side
    column = lax.rem(part, side)
    reach = RING // 2
    blocks = 2 * reach * side + side

    def device_at(steps, other):
        return lax.rem(level + steps + RING, RING) * side + other

    def block_at(way, steps, other):
        return (way * reach + steps) * side + other

    barrier = pltpu.get_barrier_semaphore()

    def group_peer(d):
        return lax.rem(me + d, groups)

    def greet_group(d, carry):
        to = group_peer(d)

        @pl.when(to != 0)
        def _():
            pl.semaphore_signal(barrier, inc=1, device_id=(to, part), device_id_type=MESH)

        return carry

    def greet_part(d, carry):
        to = device_at(d // side - reach + 1, lax.rem(d, side))

        @pl.when(to != part)
        def _():
            pl.semaphore_signal(barrier, inc=1, device_id=(0, to), device_id_type=MESH)

        return carry

    def tell_group(d, carry):
        pl.semaphore_signal(go_sem, inc=1, device_id=(d, part), device_id_type=MESH)
        return carry

    others_near = (2 * reach - 1) * side - 1
    lax.fori_loop(1, groups, greet_group, 0)

    loads = [
        pltpu.make_async_copy(source, target, load_sem.at[i])
        for i, (source, target) in enumerate(
            (
                *(
                    (x_hbm.at[c, pl.ds(r, 16)], x_v.at[c, pl.ds(r, 16)])
                    for c in range(3)
                    for r in range(0, coefs, 16)
                ),
                (send_point_hbm, send_point),
                (dest_node_hbm, dest_node),
                (pair_counts_hbm, pair_counts),
                (metrics_hbm, metrics),
                (base_hbm, base_v),
                (grad_hbm, grad_tables),
                (dz_hbm, dz),
                (synth_high_hbm, synth_high),
                (synth_low_hbm, synth_low),
                (analysis_high_hbm, analysis_high),
                (analysis_low_hbm, analysis_low),
            )
        )
    ]
    cuts = 3 * coefs // 16
    for load in loads[:cuts]:
        load.start()

    for n, (_, _, count, _, upward) in enumerate(CHUNKS):
        for other in range(side):
            if upward < count // 2:
                recv_slots[n][block_at(UP, reach - 1, other), upward : count // 2, :] = jnp.zeros(
                    (count // 2 - upward, 128), F32
                )
            if upward:
                recv_slots[n][block_at(DOWN, reach - 1, other), 0:upward, :] = jnp.zeros(
                    (upward, 128), F32
                )
    for load in loads[:cuts]:
        load.wait()
    for load in loads[cuts:]:
        load.start()
    loads = loads[cuts:]
    for g in range(groups):
        first = g * points
        stage_a[g, :, 0:128] = x_v[0, :, first : first + 128]
        rest = [x_v[c, :, first + 128 : first + points] for c in range(3)]
        rest.append(jnp.zeros((coefs, 128 - 3 * extra), F32))
        stage_a[g, :, 128:256] = jnp.concatenate(rest, axis=1)

    @pl.when(me != 0)
    def _():
        pl.semaphore_wait(barrier, groups - 1)
        pl.semaphore_signal(ready_sem, inc=1, device_id=(0, part), device_id_type=MESH)

    @pl.when(me == 0)
    def _():
        pl.semaphore_wait(ready_sem, groups - 1)
        lax.fori_loop(0, others_near + 1, greet_part, 0)

    def group_copy(source, target, send, recv, to):
        return pltpu.make_async_remote_copy(
            src_ref=source,
            dst_ref=target,
            send_sem=send,
            recv_sem=recv,
            device_id=(to, part),
            device_id_type=MESH,
        )

    def group_all(room, send, recv):
        whole = room.at[pl.ds(0, groups - 1)]
        return group_copy(whole, whole, send, recv, me)

    def send_a(d, carry):
        to = group_peer(d)
        group_copy(stage_a.at[to], coef_a.at[me], a_send, a_recv, to).start()
        return carry

    def send_b(d, carry):
        to = group_peer(d)
        group_copy(stage_b.at[to], coef_b.at[me], b_send, b_recv, to).start()
        return carry

    lax.fori_loop(1, groups, send_a, 0)
    for g in range(groups):
        first = g * points
        stage_b[g, :, 0:128] = x_v[1, :, first : first + 128]
        stage_b[g, :, 128:256] = x_v[2, :, first : first + 128]
    lax.fori_loop(1, groups, send_b, 0)
    coef_a[me] = stage_a[me]
    coef_b[me] = stage_b[me]

    for load in loads[0:3]:
        load.wait()
    owner_idx = lax.broadcasted_iota(jnp.int32, (partners, 64), 0)
    slot_idx = lax.broadcasted_iota(jnp.int32, (partners, 64), 1)
    live = jnp.zeros((partners, 64), jnp.int32)
    for o in range(partners):
        live = jnp.where(owner_idx == o, pair_counts[0, o], live)
    live = slot_idx < live
    wanted = jnp.where(live, send_point[0], -1)
    fed = jnp.where(live, dest_node[0], -1).astype(F32)
    for o in range(partners):
        half = o % 2 * 64
        picks[o // 2 : o // 2 + 1, half : half + 64] = wanted[o : o + 1]
        nodes[o, :, 0:64] = fed[o : o + 1]
        nodes[o, :, 64:128] = fed[o : o + 1]

    def part_copy(source, target, send, recv, to):
        return pltpu.make_async_remote_copy(
            src_ref=source,
            dst_ref=target,
            send_sem=send,
            recv_sem=recv,
            device_id=(me, to),
            device_id_type=MESH,
        )

    def each_other(steps, act):
        def step(d, carry):
            act(lax.rem(column + d, side))
            return carry

        lax.fori_loop(0 if steps else 1, side, step, 0)

    def node_copy(way, steps, distance, other):
        landed = block_at(way, steps, column)
        to = device_at(-steps if way == DOWN else steps, other)
        owner = device_at(distance, other)
        return part_copy(
            nodes.at[owner], node_in.at[landed], node_send, node_recv, to
        )

    node_whole = node_in.at[pl.ds(0, blocks - 3)]
    node_all = part_copy(node_whole, node_whole, node_send, node_recv, part)

    for load in loads[3:7]:
        load.wait()
    lane_points = lax.broadcasted_iota(jnp.int32, (1, 256), 1)
    first_elem = me * (points // (NP * NP))

    def metric_row(r):
        row = jnp.zeros((1, 256), F32)
        for e in range(points // (NP * NP)):
            row = jnp.where(lane_points >= e * NP * NP, metrics[r, first_elem + e], row)
        return row

    for half in range(2):
        grad = grad_tables[0] * metric_row(2 * half) + grad_tables[1] * metric_row(2 * half + 1)
        high, low = split(grad)
        grad_high[:, half * 256 : half * 256 + 256] = high
        grad_low[:, half * 256 : half * 256 + 256] = low
        vel_xy[0:256, half * 256 : half * 256 + 256] = grad
    padded[128:256, :] = jnp.zeros((128, planes), F32)

    def base_step(c, carry):
        padded[0:points, :] = base_v[c, :, 0, :]
        base_t[c] = jnp.transpose(padded[...])
        base_z[c] = dot6(dz[...], base_t[c])
        flow_xy[c] = dot6(base_t[c], vel_xy[0:256, :])
        return carry

    lax.fori_loop(0, 3, base_step, 0)

    rows = pick_table.shape[0]
    point_idx = lax.broadcasted_iota(jnp.int32, (rows, 128), 0)

    def pick_step(j, carry, place, distance):
        wanted = picks[pl.ds(lax.rem(level + distance, RING) * (side // 2) + j, 1), :]
        columns = pl.ds(pl.multiple_of((place * (side // 2) + j) * 128, 128), 128)
        pick_table[:, columns] = jnp.where(point_idx == wanted, 1.0, 0.0).astype(BF16)
        return carry

    for place, distance in enumerate(DISTANCES):
        lax.fori_loop(
            0, side // 2, lambda j, c, p=place, d=distance: pick_step(j, c, p, d), 0
        )

    @pl.when(me == 0)
    def _():
        pl.semaphore_wait(barrier, others_near)
        lax.fori_loop(1, groups, tell_group, 0)

    @pl.when(me != 0)
    def _():
        pl.semaphore_wait(go_sem, 1)

    for distance in DISTANCES:
        for way, steps in routes(distance):
            each_other(
                steps,
                lambda other, w=way, s=steps, d=distance: node_copy(w, s, d, other).start(),
            )
            if steps == 0:
                node_in[block_at(way, steps, column)] = nodes[device_at(distance, column)]

    lane = lax.broadcasted_iota(jnp.int32, (1, 128), 1)
    left = lane < 64
    adv_parts[:, rows - 128 : rows] = jnp.zeros((2 * coefs, 128), BF16)

    for load in loads[7:]:
        load.wait()

    group_all(coef_a, a_send, a_recv).wait_recv()
    high, low = split(coef_a[...].reshape(planes, 256))
    both = dot3(synth_high[...], synth_low[...], high, low)
    vel[0, :, 0:128] = both[0:planes, 0:128]
    along_z[0, :, 0:128] = both[planes : 2 * planes, 0:128]
    for c in range(3):
        rest = both[:, 128:256]
        if c:
            rest = pltpu.roll(rest, 128 - c * extra, 1)
        rest = jnp.where(lane < extra, rest, 0.0)
        vel[c, :, 128:256] = rest[0:planes]
        along_z[c, :, 128:256] = rest[planes : 2 * planes]

    block = 32

    def first_pass(i):
        high, low = split(vel[i])
        vel_xy[...] = dot3(high, low, grad_high[...], grad_low[...])

        def point_step(b, carry):
            at = pl.ds(pl.multiple_of(b * block, block), block)
            total = vel[i, at, :] * flow_back(i, i, at)
            for j in range(3):
                slope = along_z[i, at, :] if j == 2 else vel_xy[at, j * 256 : j * 256 + 256]
                total = total - base_t[j, at, :] * slope
            adv[at, :] = total
            return carry

        lax.fori_loop(0, planes // block, point_step, 0)

    def flow_back(i, j, at):
        return base_z[j, at, :] if i == 2 else flow_xy[j, at, i * 256 : i * 256 + 256]

    first_pass(0)
    group_all(coef_b, b_send, b_recv).wait_recv()

    def second_half(rows, target):
        high, low = split(coef_b[...].reshape(planes, 256))
        part_b = dot3(synth_high[rows, :], synth_low[rows, :], high, low)
        target[1, :, 0:128] = part_b[:, 0:128]
        target[2, :, 0:128] = part_b[:, 128:256]

    second_half(slice(0, planes), vel)

    def advect(i):
        if i:
            first_pass(i)

        def point_step(b, carry):
            at = pl.ds(pl.multiple_of(b * block, block), block)
            total = adv[at, :]
            for j in range(3):
                if j != i:
                    total = total + vel[j, at, :] * flow_back(i, j, at)
            high, low = split(total)
            phys_high[at, :] = high
            phys_low[at, :] = low
            return carry

        lax.fori_loop(0, planes // block, point_step, 0)
        adv[...] = dot3(analysis_high[...], analysis_low[...], phys_high[...], phys_low[...])

    def back_copy(n, to):
        return group_copy(
            send_adv[n].at[to], recv_adv[n].at[me], adv_send.at[n], adv_recv.at[n], to
        )

    def send_back(n):
        _, start, count, fold, _ = CHUNKS[n]
        packed = packed_rows(count, fold)
        for m in range(groups):
            at = m * coefs + start
            send_adv[n][m, 0:count, :] = adv[at : at + count, 0:128]
            rest = adv[at : at + count, 128:256]
            merged = rest[:packed]
            for f in range(1, fold):
                piece = rest[f * packed : min((f + 1) * packed, count)]
                if piece.shape[0] < packed:
                    filler = jnp.zeros((packed - piece.shape[0], 128), F32)
                    piece = jnp.concatenate([piece, filler], axis=0)
                merged = jnp.where(lane < f * extra, merged, pltpu.roll(piece, f * extra, 1))
            send_adv[n][m, count : count + packed, :] = merged

        def step(d, carry):
            back_copy(n, group_peer(d)).start()
            return carry

        lax.fori_loop(1, groups, step, 0)
        recv_adv[n][me] = send_adv[n][me]

    stores = []

    def late_slopes():
        second_half(slice(planes, 2 * planes), along_z)

    def way_rows(n, way, steps):
        _, _, count, _, upward = CHUNKS[n]
        if steps < reach - 1 or way == HERE:
            return 0, count // 2
        return (0, upward) if way == UP else (upward, count // 2 - upward)

    def slot_copy(n, way, steps, distance, other):
        first, rows_sent = way_rows(n, way, steps)
        landed = block_at(way, steps, column)
        place = DISTANCES.index(distance) * side + other
        return part_copy(
            send_slots[n].at[place, pl.ds(first, rows_sent)],
            recv_slots[n].at[landed, pl.ds(first, rows_sent)],
            slot_send.at[n],
            slot_recv.at[int(way == HERE), n],
            device_at(-steps if way == DOWN else steps, other),
        )

    summed_here = 2 * (reach - 2) * side + side + 2 * (side - 1)

    def slots_all(n, count, here):
        whole = recv_slots[n].at[pl.ds(0, count)]
        return part_copy(whole, whole, slot_send.at[n], slot_recv.at[here, n], part)

    def each_slot_copy(n, distance, act):
        for way, steps in routes(distance):
            if way_rows(n, way, steps)[1]:
                each_other(
                    steps,
                    lambda other, w=way, s=steps: act(slot_copy(n, w, s, distance, other)),
                )

    def dense_copy(n, way):
        return part_copy(
            dense.at[way, n, pl.ds(0, CHUNKS[n][2])],
            dense_in.at[way, n, pl.ds(0, CHUNKS[n][2])],
            dense_send.at[way, n],
            dense_recv.at[way, n],
            device_at(1 if way == UP else -1, column),
        )

    wide = min(512, 128 * pairs)
    tiles = 128 * pairs // wide
    tile_owners = 2 * (wide // 128)

    def send_picked(n):
        i, start, count, fold, _ = CHUNKS[n]
        packed = packed_rows(count, fold)

        group_all(recv_adv[n], adv_send.at[n], adv_recv.at[n]).wait_recv()
        for g in range(groups):
            first = g * points
            rest = recv_adv[n][g, count : count + packed, :]
            pieces = [rest]
            for f in range(1, fold):
                piece = pltpu.roll(rest, 128 - f * extra, 1)
                pieces.append(piece[: min(packed, count - f * packed)])
            rest = jnp.concatenate(pieces, axis=0)
            advection[i, start : start + count, first : first + 128] = recv_adv[n][g, 0:count, :]
            advection[i, start : start + count, first + 128 : first + points] = rest[:, :extra]
        store = pltpu.make_async_copy(
            advection.at[i, pl.ds(start, count)],
            advection_hbm.at[i, pl.ds(start, count)],
            store_sem.at[n],
        )
        store.start()
        stores.append(store)
        high, low = split(advection[i, start : start + count, :])
        adv_parts[0:count, 0:full] = high
        adv_parts[count : 2 * count, 0:full] = low
        half = count // 2

        for t in range(tiles):
            picked = dot(adv_parts[0 : 2 * count, :], pick_table[:, t * wide : (t + 1) * wide])
            picked = picked[0:count] + picked[count : 2 * count]
            for j in range(wide // 128):
                upper = picked[0:half, j * 128 : j * 128 + 128]
                lower = picked[half:count, j * 128 : j * 128 + 128]
                place = t * tile_owners + 2 * j
                send_slots[n][place] = jnp.where(left, upper, pltpu.roll(lower, 64, 1))
                send_slots[n][place + 1] = jnp.where(left, pltpu.roll(upper, 64, 1), lower)
            for place in range(t * tile_owners // side, (t + 1) * tile_owners // side):
                distance = DISTANCES[place]
                each_slot_copy(n, distance, lambda copy: copy.start())
                for way, steps in routes(distance):
                    if steps == 0:
                        recv_slots[n][block_at(way, steps, column)] = send_slots[n][
                            place * side + column
                        ]

    def sum_blocks(n, first, last):
        count = CHUNKS[n][2]
        for j in range(first // 2, last // 2):
            even = recv_slots[n][2 * j]
            odd = recv_slots[n][2 * j + 1]
            upper = jnp.where(left, even, pltpu.roll(odd, 64, 1))
            lower = jnp.where(left, pltpu.roll(even, 64, 1), odd)
            high, low = split(jnp.concatenate([upper, lower], axis=0))
            slot_parts[0:count, j * 128 : j * 128 + 128] = high
            slot_parts[count : 2 * count, j * 128 : j * 128 + 128] = low
        summed = dot(
            slot_parts[0 : 2 * count, 64 * first : 64 * last], node_table[64 * first : 64 * last, :]
        )
        return summed[0:count] + summed[count : 2 * count]

    def fill_node_table():
        node_all.wait_recv()
        node_rows[...] = jnp.zeros((128, 128), F32)
        for j in range(blocks // 2):
            node_rows[j : j + 1, :] = jnp.where(left, node_in[2 * j], node_in[2 * j + 1])
        node_columns = jnp.transpose(node_rows[...])
        node_idx = lax.broadcasted_iota(jnp.int32, (128, NODES_OWN), 1).astype(F32)
        for j in range(blocks // 2):
            node_table[128 * j : 128 * j + 128, :] = jnp.where(
                node_idx == node_columns[:, j : j + 1], 1.0, 0.0
            ).astype(BF16)

    def pass_on(n):
        count = CHUNKS[n][2]
        slots_all(n, summed_here, 0).wait_recv()
        for way in (UP, DOWN):
            dense[way, n, 0:count, :] = sum_blocks(
                n, way * reach * side, (way + 1) * reach * side
            )
            dense_copy(n, way).start()

    def add_nodes(n):
        i, start, count, _, _ = CHUNKS[n]
        slots_all(n, side - 1, 1).wait_recv()
        here = sum_blocks(n, 2 * reach * side, blocks)
        for way in (UP, DOWN):
            dense_copy(n, way).wait_recv()
        totals[i, start : start + count, :] = (
            here + dense_in[UP, n, 0:count, :] + dense_in[DOWN, n, 0:count, :]
        )
        store = pltpu.make_async_copy(
            totals.at[i, pl.ds(start, count)],
            totals_hbm.at[i, pl.ds(start, count)],
            store_sem.at[len(CHUNKS) + n],
        )
        store.start()
        stores.append(store)

    advect(0)
    send_back(0)
    send_back(1)
    late_slopes()
    advect(1)
    send_back(2)
    send_picked(0)
    advect(2)
    send_back(3)
    send_picked(1)
    send_picked(2)
    send_picked(3)
    fill_node_table()
    pass_on(0)
    pass_on(1)
    pass_on(2)
    pass_on(3)
    add_nodes(0)
    add_nodes(1)
    add_nodes(2)
    add_nodes(3)

    group_all(stage_a, a_send, a_recv).wait_send()
    group_all(stage_b, b_send, b_recv).wait_send()
    for n in range(len(CHUNKS)):
        group_all(send_adv[n], adv_send.at[n], adv_recv.at[n]).wait_send()
    node_all.wait_send()
    for n in range(len(CHUNKS)):
        slots_all(n, summed_here + side - 1, 0).wait_send()
    for n in range(len(CHUNKS)):
        for way in (UP, DOWN):
            dense_copy(n, way).wait_send()
    for store in stores:
        store.wait()


def per_device(adjoint_modes, base_planes, metrics, send_point, dest_node, pair_counts):
    components, coefs, local_points = adjoint_modes.shape
    planes = base_planes.shape[3]
    groups = lax.axis_size("modes")
    partners = lax.axis_size("elems")
    points = local_points // groups
    pairs = partners // 2
    synth, analysis, slope, dz = spectral_tables(planes)
    synth_high, synth_low = halves_of(np.concatenate([synth, slope], axis=0))
    analysis_high, analysis_low = halves_of(analysis)
    grad = gradient_tables(points // (NP * NP), 256)

    rows = -(-local_points // 128) * 128
    blocks = partners + partners // RING
    any_spec = pl.BlockSpec(memory_space=pl.ANY)

    def room(*shape, dtype=F32):
        return pltpu.VMEM(shape, dtype)

    dma = pltpu.SemaphoreType.DMA
    scratch = [
        room(3, coefs, local_points),
        room(3, points, 1, planes),
        pltpu.SMEM(metrics.shape, F32),
        room(*send_point.shape, dtype=jnp.int32),
        room(*dest_node.shape, dtype=jnp.int32),
        pltpu.SMEM(pair_counts.shape, jnp.int32),
        room(2 * planes, planes, dtype=BF16),
        room(2 * planes, planes, dtype=BF16),
        room(planes, planes),
        room(planes, planes, dtype=BF16),
        room(planes, planes, dtype=BF16),
        room(2, 256, 256),
        room(groups, coefs, 256),
        room(groups, coefs, 256),
        room(groups, coefs, 256),
        room(groups, coefs, 256),
        room(256, planes),
        room(3, planes, 256),
        room(3, planes, 256),
        room(3, planes, 512),
        room(256, 512, dtype=BF16),
        room(256, 512, dtype=BF16),
        room(pairs, 128, dtype=jnp.int32),
        room(partners, 1, 128),
        room(rows, pairs * 128, dtype=BF16),
        room(128, 128),
        room(blocks * 64, NODES_OWN, dtype=BF16),
        room(blocks, 1, 128),
        room(3, planes, 256),
        room(3, planes, 256),
        room(planes, 512),
        room(planes, 256, dtype=BF16),
        room(planes, 256, dtype=BF16),
        room(planes, 256),
        room(3, coefs, local_points),
        room(2 * coefs, rows, dtype=BF16),
        room(2 * coefs, blocks * 64, dtype=BF16),
        room(3, coefs, NODES_OWN),
        room(2, len(CHUNKS), coefs, NODES_OWN),
        room(2, len(CHUNKS), coefs, NODES_OWN),
        dma((11 + 3 * coefs // 16,)),
        dma((2 * len(CHUNKS),)),
        dma,
        dma,
        dma,
        dma,
        dma((len(CHUNKS),)),
        dma((len(CHUNKS),)),
        dma,
        dma,
        dma((len(CHUNKS),)),
        dma((2, len(CHUNKS))),
        dma((2, len(CHUNKS))),
        dma((2, len(CHUNKS))),
        pltpu.SemaphoreType.REGULAR,
        pltpu.SemaphoreType.REGULAR,
    ]
    for _ in range(2):
        for _, _, count, fold, _ in CHUNKS:
            scratch.append(room(groups, count + packed_rows(count, fold), 128))
    for received in (False, True):
        for _, _, count, _, _ in CHUNKS:
            scratch.append(room(blocks if received else partners, count // 2, 128))

    def kernel(*refs):
        body(groups, partners, points, *refs)

    results = pl.pallas_call(
        kernel,
        out_shape=(
            jax.ShapeDtypeStruct((3, coefs, local_points), F32),
            jax.ShapeDtypeStruct((3, coefs, NODES_OWN), F32),
        ),
        in_specs=[any_spec] * 12,
        out_specs=(any_spec, any_spec),
        scratch_shapes=scratch,
        compiler_params=pltpu.CompilerParams(
            collective_id=0, has_side_effects=True, vmem_limit_bytes=56 * 1024 * 1024
        ),
    )(
        adjoint_modes,
        jnp.transpose(base_planes, (0, 2, 1, 3)),
        metrics,
        send_point,
        dest_node,
        pair_counts,
        synth_high,
        synth_low,
        jnp.asarray(dz, dtype=F32),
        analysis_high,
        analysis_low,
        grad,
    )

    def hand_over(advection, totals, advection_out, totals_out, held, held_totals, sem_in, sem_out):
        pieces = [
            tuple(room.at[c, pl.ds(r, coefs // CUTS)] for room in rooms)
            for rooms in ((advection, held, advection_out), (totals, held_totals, totals_out))
            for c in range(components)
            for r in range(0, coefs, coefs // CUTS)
        ]
        loads = [
            pltpu.make_async_copy(source, middle, sem_in.at[i])
            for i, (source, middle, _) in enumerate(pieces)
        ]
        stores = [
            pltpu.make_async_copy(middle, target, sem_out.at[i])
            for i, (_, middle, target) in enumerate(pieces)
        ]
        for load in loads:
            load.start()
        for load, store in zip(loads, stores):
            load.wait()
            store.start()
        for store in stores:
            store.wait()

    return pl.pallas_call(
        hand_over,
        out_shape=tuple(jax.ShapeDtypeStruct(r.shape, r.dtype) for r in results),
        in_specs=[any_spec, any_spec],
        out_specs=(any_spec, any_spec),
        scratch_shapes=[room(*r.shape) for r in results] + [dma((2 * components * CUTS,))] * 2,
        compiler_params=pltpu.CompilerParams(vmem_limit_bytes=56 * 1024 * 1024),
    )(*results)


def solution(mesh):
    return jax.shard_map(
        per_device,
        mesh=mesh,
        in_specs=(
            P(None, "modes", "elems"),
            P(None, "modes", "elems", None),
            P(None, "elems"),
            P("elems", None, None),
            P("elems", None, None),
            P("elems", None),
        ),
        out_specs=(P(None, "modes", "elems"), P(None, "modes", "elems")),
        check_vma=False,
    )
```
